128 devices in a mesh: fsdp: 16 (over x_lo, y, core), dp: 8 (over x_hi, z).
Axes of the slice: x: 4 (x_hi: 2, x_lo: 2; x = x_hi * 2 + x_lo), y: 4, z: 4, core: 2. Of those that a mesh axis runs over, the one named last changes fastest.
Arguments:
- tokens: bfloat16 [16, 1024, 2048], P('fsdp', 'dp'), may hold values from -6 to 6
- segment_ids: int32 [16, 1024], P('fsdp'), may hold values from -1 to 2, as said below
- out_cotangent: bfloat16 [16, 1024, 2048], P('fsdp', 'dp'), may hold values from -6 to 6
- ln1_gain: bfloat16 [2048], P('fsdp'), may hold values from 0.5 to 1.5
- ln1_bias: bfloat16 [2048], P('fsdp'), may hold values from -1.1953125 to 1.1953125
- qkv_weight: bfloat16 [2048, 6144], P('fsdp'), may hold values from -0.125 to 0.125
- qkv_bias: bfloat16 [6144], P('fsdp'), may hold values from -0.59765625 to 0.59765625
- out_weight: bfloat16 [2048, 2048], P('fsdp'), may hold values from -1 to 1
- out_bias: bfloat16 [2048], P('fsdp'), may hold values from -1.1953125 to 1.1953125
- ln2_gain: bfloat16 [2048], P('fsdp'), may hold values from 0.5 to 1.5
- ln2_bias: bfloat16 [2048], P('fsdp'), may hold values from -1.1953125 to 1.1953125
- up_weight: bfloat16 [2048, 8192], P('fsdp'), may hold values from -0.125 to 0.125
- up_bias: bfloat16 [8192], P('fsdp'), may hold values from -1.1953125 to 1.1953125
- down_weight: bfloat16 [8192, 2048], P('fsdp'), may hold values from -0.0625 to 0.0625
- down_bias: bfloat16 [2048], P('fsdp'), may hold values from -1.1953125 to 1.1953125
Outputs:
- layer_output: bfloat16 [16, 1024, 2048], P('fsdp', 'dp')
- input_grad: bfloat16 [16, 1024, 2048], P('fsdp', 'dp')
- grad_ln1_gain: float32 [2048], P('fsdp')
- grad_ln1_bias: float32 [2048], P('fsdp')
- grad_qkv_weight: float32 [2048, 6144], P('fsdp')
- grad_qkv_bias: float32 [6144], P('fsdp')
- grad_out_weight: float32 [2048, 2048], P('fsdp')
- grad_out_bias: float32 [2048], P('fsdp')
- grad_ln2_gain: float32 [2048], P('fsdp')
- grad_ln2_bias: float32 [2048], P('fsdp')
- grad_up_weight: float32 [2048, 8192], P('fsdp')
- grad_up_bias: float32 [8192], P('fsdp')
- grad_down_weight: float32 [8192, 2048], P('fsdp')
- grad_down_bias: float32 [2048], P('fsdp')
The draws below stay inside these ranges and needn't reach their ends.
Inputs may be any that keep to these rules, and one draw needn't show every extreme that they name: `segment_ids`: each packed sequence holds, in order, document 0 of fewer than 128 positions, document 1, document 2 of fewer than 64 positions, and fewer than 64 padding positions marked -1; each of the four runs is nonempty.
All inputs are finite; a program needn't handle non-finite values.
Results may differ from the reference program's by a relative error of at most 0.02.
Values may be sent and summed in bfloat16 or wider, within the bound.
No kernel may reach another device: no remote copies, remote signals or barrier semaphores. Data moves between devices by JAX's collectives and lax.ppermute only.
A program may use at most 448 MiB of HBM per device.

```python
import math
import jax
import jax.numpy as jnp
from jax import lax

D = 2048
FF = 8192
HEADS = 8
ROTARY = 64
SEQ = 1024
SHARD = 128
BATCH = 16


def draw_segment_ids(key, part):
    key = jax.random.fold_in(key, 7)
    key_head, key_pad, key_tail = jax.random.split(key, 3)
    head_len = jax.random.randint(key_head, (BATCH, 1), 1, SHARD)
    pad_len = jax.random.randint(key_pad, (BATCH, 1), 1, SHARD // 2)
    tail_len = jax.random.randint(key_tail, (BATCH, 1), 1, SHARD // 2)
    places = jnp.arange(SEQ, dtype=jnp.int32)[None, :]
    long_end = SEQ - pad_len - tail_len
    return jnp.where(places < head_len, 0, jnp.where(places < long_end, 1, jnp.where(places < SEQ - pad_len, 2, -1))).astype(jnp.int32)


def steps_of(key, extent, cuts, low, largest):
    def one(axis_at, parts):
        steps = jax.random.uniform(jax.random.fold_in(jax.random.fold_in(key, 6), axis_at), (parts,), jnp.float32, low / len(cuts), largest / len(cuts))
        return jnp.repeat(jnp.exp(steps), extent[axis_at] // parts).reshape((-1,) + (1,) * (len(extent) - axis_at - 1))

    gain = one(*cuts[0])
    for cut in cuts[1:]:
        gain = gain * one(*cut)
    return gain


def bell_draw(key, extent, scale, limit, cuts=(), held_as=jnp.bfloat16):
    values = scale * jax.random.normal(key, extent, jnp.float32)
    if cuts:
        values = values * steps_of(key, extent, cuts, -0.22, 0.18)
    return jnp.clip(values, -limit, limit).astype(held_as)


def setup_inputs(seed: int = 0) -> dict:
    seeds = jax.random.split(jax.random.key(seed), 16)
    return {
        "tokens": bell_draw(seeds[0], (BATCH, SEQ, D), 1.0, 6.0, ((0, 16), (1, 8))),
        "segment_ids": draw_segment_ids(jax.random.fold_in(seeds[15], 71), 0),
        "out_cotangent": bell_draw(seeds[2], (BATCH, SEQ, D), 1.0, 6.0, ((0, 16), (1, 8))),
        "ln1_gain": jnp.clip(1.0 + 0.1 * jax.random.normal(seeds[3], (D,), jnp.float32), 0.5, 1.5).astype(jnp.bfloat16),
        "ln1_bias": bell_draw(seeds[4], (D,), 0.2, 1.1953125, ((0, 16),)),
        "qkv_weight": bell_draw(seeds[5], (D, 3 * D), D ** -0.5, 0.125, ((0, 16),)),
        "qkv_bias": bell_draw(seeds[6], (3 * D,), 0.1, 0.59765625, ((0, 16),)),
        "out_weight": bell_draw(seeds[7], (D, D), (D // 64) ** -0.5, 1.0, ((0, 16),)),
        "out_bias": bell_draw(seeds[8], (D,), 0.2, 1.1953125, ((0, 16),)),
        "ln2_gain": jnp.clip(1.0 + 0.1 * jax.random.normal(seeds[9], (D,), jnp.float32), 0.5, 1.5).astype(jnp.bfloat16),
        "ln2_bias": bell_draw(seeds[10], (D,), 0.2, 1.1953125, ((0, 16),)),
        "up_weight": bell_draw(seeds[11], (D, FF), D ** -0.5, 0.125, ((0, 16),)),
        "up_bias": bell_draw(seeds[12], (FF,), 0.2, 1.1953125, ((0, 16),)),
        "down_weight": bell_draw(seeds[13], (FF, D), FF ** -0.5, 0.0625, ((0, 16),)),
        "down_bias": bell_draw(seeds[14], (D,), 0.2, 1.1953125, ((0, 16),)),
    }


norm_eps = 1e-05
masked_score = -1e+30

@jax.custom_vjp
def low(v):
    return lax.optimization_barrier(v.astype(jnp.bfloat16)).astype(jnp.float32)

@jax.custom_vjp
def low_back(v):
    return v

def low_keep(v):
    return (low(v), None)

def low_pass(kept, grad):
    return (grad,)

def back_keep(v):
    return (v, None)

def back_low(kept, grad):
    return (low(grad),)
low.defvjp(low_keep, low_pass)
low_back.defvjp(back_keep, back_low)

def layer_norm(values, gain_vec, shift_vec):
    center = values - lax.optimization_barrier(jnp.mean(values, axis=-1, keepdims=True))
    spread = lax.optimization_barrier(jnp.mean(center * center, axis=-1, keepdims=True))
    return center * lax.rsqrt(spread + norm_eps) * gain_vec + shift_vec

def rotary_tables(places, rotary):
    half_dims = rotary // 2
    freqs = jnp.exp(jnp.arange(half_dims, dtype=jnp.float32) * (-2.0 * math.log(10000.0) / rotary))
    angles = places.astype(jnp.float32)[:, None] * freqs[None, :]
    return (jnp.cos(angles), jnp.sin(angles))

def rotate(head_vals, rot_cos, rot_sin, rotary):
    half_dims = rotary // 2
    front_half = head_vals[..., :half_dims]
    back_half = head_vals[..., half_dims:rotary]
    return jnp.concatenate([front_half * rot_cos - back_half * rot_sin, back_half * rot_cos + front_half * rot_sin, head_vals[..., rotary:]], axis=-1)

def forward(params, inputs, doc_ids):
    gain_one, bias_one, w_qkv, b_qkv, w_out, b_out, gain_two, bias_two, w_up, b_up, w_down, b_down = params
    seq_len, model_width = inputs.shape
    head_dim = model_width // HEADS
    highest = lax.Precision.HIGHEST
    places = jnp.arange(seq_len, dtype=jnp.int32)
    rot_cos, rot_sin = rotary_tables(places, ROTARY)
    rot_cos = rot_cos[:, None, :]
    rot_sin = rot_sin[:, None, :]
    normed_one = low(layer_norm(inputs, gain_one, bias_one))
    mixed = low_back(jnp.dot(normed_one, w_qkv, precision=highest) + b_qkv)
    query = low(rotate(mixed[:, :model_width].reshape(seq_len, HEADS, head_dim), rot_cos, rot_sin, ROTARY))
    key_vals = low(rotate(mixed[:, model_width:2 * model_width].reshape(seq_len, HEADS, head_dim), rot_cos, rot_sin, ROTARY))
    value_vals = low(mixed[:, 2 * model_width:].reshape(seq_len, HEADS, head_dim))
    scores = low_back(jnp.einsum('qhd,khd->hqk', query, key_vals, precision=highest) * head_dim ** (-0.5))
    allowed = (doc_ids[:, None] == doc_ids[None, :]) & (doc_ids[None, :] >= 0) & (places[None, :] <= places[:, None]) | (places[None, :] == places[:, None])
    scores = jnp.where(allowed[None], scores, masked_score)
    prob = low(jax.nn.softmax(scores, axis=-1))
    attended = low_back(low(jnp.einsum('hqk,khd->qhd', prob, value_vals, precision=highest).reshape(seq_len, model_width)))
    branch_attn = jnp.dot(attended, w_out, precision=highest) + b_out
    normed_two = low(layer_norm(inputs, gain_two, bias_two))
    pre_act = low_back(jnp.dot(normed_two, w_up, precision=highest) + b_up)
    activ = low(jax.nn.gelu(pre_act, approximate=False))
    branch_ffn = jnp.dot(activ, w_down, precision=highest) + b_down
    return inputs + branch_attn + branch_ffn

def reference(tokens, segment_ids, out_cotangent, ln1_gain, ln1_bias, qkv_weight, qkv_bias, out_weight, out_bias, ln2_gain, ln2_bias, up_weight, up_bias, down_weight, down_bias):
    params = tuple((item.astype(jnp.float32) for item in (ln1_gain, ln1_bias, qkv_weight, qkv_bias, out_weight, out_bias, ln2_gain, ln2_bias, up_weight, up_bias, down_weight, down_bias)))

    def one_pack(grads, pack):
        pack_rows, pack_ids, pack_cot = pack

        def apply_layer(prm, inputs):
            return forward(prm, inputs, pack_ids)
        result, backward = jax.vjp(apply_layer, params, pack_rows.astype(jnp.float32))
        param_grads, input_grads = backward(pack_cot.astype(jnp.float32))
        grads = jax.tree.map(jnp.add, grads, param_grads)
        return (grads, (result.astype(jnp.bfloat16), input_grads.astype(jnp.bfloat16)))
    zero_grads = jax.tree.map(jnp.zeros_like, params)
    grads, (outputs, input_grads) = lax.scan(one_pack, zero_grads, (tokens, segment_ids, out_cotangent))
    return (outputs, input_grads, grads[0], grads[1], grads[2], grads[3], grads[4], grads[5], grads[6], grads[7], grads[8], grads[9], grads[10], grads[11])
```

```python
import math

import jax
import jax.numpy as jnp
from jax import lax
from jax.sharding import Mesh, PartitionSpec as P

HEADS = 8
ROTARY = 64
NORM_EPS = 1e-05
MASKED = -1e30
BF = jnp.bfloat16
F32 = jnp.float32
CHIPS = ("x", "y")
COPIES = ("w", "z")


def block_moves():
    moves = []
    for x in range(2):
        for y in range(4):
            for w in range(2):
                for z in range(4):
                    source = ((x * 4 + y) * 2 + w) * 4 + z
                    target = ((w * 4 + (y + z) % 4) * 2 + x) * 4 + y
                    moves.append((source, target))
    return moves


MOVES = block_moves()
BACK = [(target, source) for source, target in MOVES]


def move(block, pairs):
    return lax.ppermute(block, ("x", "y", "w", "z"), pairs)


def swap_core(block):
    return lax.ppermute(block, "c", [(0, 1), (1, 0)])


def dot(a, b, dims):
    return lax.dot_general(a, b, (dims, ((), ())), preferred_element_type=F32)


def rotate(head, cos, sin):
    half = ROTARY // 2
    front, back = head[:, :half], head[:, half:ROTARY]
    return jnp.concatenate(
        [front * cos - back * sin, back * cos + front * sin, head[:, ROTARY:]], axis=1
    )


def core_pair(own, other, core, axis):
    return jnp.where(core == 0, jnp.stack([own, other], axis), jnp.stack([other, own], axis))


def core_sum(both, core, axis):
    keep = lax.dynamic_index_in_dim(both, core, axis, keepdims=False)
    give = lax.dynamic_index_in_dim(both, 1 - core, axis, keepdims=False)
    got = swap_core(give)
    return (keep.astype(F32) + got.astype(F32)).astype(BF)


def body(
    tokens, segment_ids, out_cotangent, ln1_gain, ln1_bias, qkv_weight, qkv_bias, out_weight, out_bias,
    ln2_gain, ln2_bias, up_weight, up_bias, down_weight, down_bias,
):
    _, shard, width = tokens.shape
    head_dim = width // HEADS
    ff = up_weight.shape[1]
    ff_part = ff // 8
    core = lax.axis_index("c")
    chip = lax.axis_index("x") * 4 + lax.axis_index("y")
    scale = head_dim ** -0.5

    x_own = move(tokens[0], MOVES)
    x_all = lax.all_gather(x_own, CHIPS, axis=0, tiled=True)
    ids = move(segment_ids, MOVES)[0]

    small = [ln1_gain, ln1_bias, out_bias, ln2_gain, ln2_bias, down_bias, qkv_bias, up_bias]
    small_all = lax.all_gather(jnp.concatenate(small), ("x", "y", "c"), axis=0)
    cut = width // 16
    gain_one, bias_one, b_out, gain_two, bias_two, b_down = (
        small_all[:, i * cut : (i + 1) * cut].reshape(width).astype(F32) for i in range(6)
    )
    b_qkv = small_all[:, 6 * cut : 9 * cut].reshape(3, HEADS, head_dim)
    b_qkv = lax.dynamic_index_in_dim(b_qkv, chip, 1, keepdims=False).reshape(3 * head_dim).astype(F32)
    b_up = small_all[:, 9 * cut :].reshape(8, ff_part)
    b_up = lax.dynamic_index_in_dim(b_up, chip, 0, keepdims=False).astype(F32)

    rows = qkv_weight.shape[0]
    q_cols = qkv_weight.reshape(rows, 3, HEADS, head_dim).transpose(2, 0, 1, 3).reshape(HEADS, rows, 3 * head_dim)
    q_half = lax.all_to_all(q_cols, CHIPS, 0, 0, tiled=True)
    w_qkv = core_pair(q_half, swap_core(q_half), core, 1).reshape(width, 3 * head_dim)
    u_cols = up_weight.reshape(rows, 8, ff_part).transpose(1, 0, 2)
    u_half = lax.all_to_all(u_cols, CHIPS, 0, 0, tiled=True)
    w_up = core_pair(u_half, swap_core(u_half), core, 1).reshape(width, ff_part)
    w_down = core_pair(down_weight, swap_core(down_weight), core, 0).reshape(ff_part, width)
    w_out = core_pair(out_weight, swap_core(out_weight), core, 0).reshape(head_dim, width)
    w_rows = jnp.concatenate([w_down, w_out], axis=0)

    g_own = move(out_cotangent[0], MOVES)
    g_all = lax.all_gather(g_own, CHIPS, axis=0, tiled=True)

    slot = jnp.arange(8, dtype=jnp.int32)
    block = (slot // 4) * 4 + (slot % 4 - lax.axis_index("z") + 4) % 4
    places = (block[:, None] * shard + jnp.arange(shard, dtype=jnp.int32)[None, :]).reshape(8 * shard)
    freqs = jnp.exp(jnp.arange(ROTARY // 2, dtype=F32) * (-2.0 * math.log(10000.0) / ROTARY))
    angles = places.astype(F32)[:, None] * freqs[None, :]
    cos, sin = jnp.cos(angles), jnp.sin(angles)
    ids_slot = jnp.take(ids.reshape(8, shard), block, axis=0).reshape(8 * shard)

    xf = x_all.astype(F32)
    center = xf - jnp.mean(xf, axis=-1, keepdims=True)
    rstd = lax.rsqrt(jnp.mean(center * center, axis=-1, keepdims=True) + NORM_EPS)
    xhat = center * rstd
    h1 = (xhat * gain_one + bias_one).astype(BF)
    h2 = (xhat * gain_two + bias_two).astype(BF)
    mixed = dot(h1, w_qkv, ((1,), (0,))) + b_qkv
    query = rotate(mixed[:, :head_dim], cos, sin).astype(BF)
    key = rotate(mixed[:, head_dim : 2 * head_dim], cos, sin).astype(BF)
    value = mixed[:, 2 * head_dim :].astype(BF)
    same = places[:, None] == places[None, :]
    allowed = (
        (ids_slot[:, None] == ids_slot[None, :]) & (ids_slot[None, :] >= 0) & (places[None, :] <= places[:, None])
    ) | same
    scores = jnp.where(allowed, dot(query, key, ((1,), (1,))) * scale, MASKED)
    expo = jnp.exp(scores - jnp.max(scores, axis=-1, keepdims=True))
    prob = expo / jnp.sum(expo, axis=-1, keepdims=True)
    prob_low = prob.astype(BF)
    attended = dot(prob_low, value, ((1,), (0,))).astype(BF)
    pre = dot(h2, w_up, ((1,), (0,))) + b_up
    act = jax.nn.gelu(pre, approximate=False).astype(BF)
    branches = jnp.concatenate([act, attended], axis=1)
    out_part = dot(branches, w_rows, ((1,), (0,))).astype(BF)
    out_sum = lax.psum_scatter(out_part, CHIPS, scatter_dimension=0, tiled=True)
    x_rows = x_own.astype(F32)
    layer_output = move((x_rows + out_sum.astype(F32) + (b_out + b_down)).astype(BF), BACK)

    g_branches = dot(g_all, w_rows, ((1,), (1,)))
    _, gelu_back = jax.vjp(lambda v: jax.nn.gelu(v, approximate=False), pre)
    g_pre = gelu_back(g_branches[:, :ff_part])[0].astype(BF)
    g_att = g_branches[:, ff_part:].astype(BF)
    grad_rows = dot(branches, g_all, ((0,), (0,))).astype(BF)
    grad_up = dot(h2, g_pre, ((0,), (0,))).astype(BF)
    grad_up_bias = jnp.sum(g_pre.astype(F32), axis=0)
    e2 = dot(g_pre, w_up, ((1,), (1,)))
    g_value = dot(prob_low, g_att, ((0,), (0,)))
    g_prob = dot(g_att, value, ((1,), (1,)))
    inner = jnp.sum(prob * g_prob, axis=-1, keepdims=True)
    g_scores = (prob * (g_prob - inner)).astype(BF)
    g_query = rotate(dot(g_scores, key, ((1,), (0,))) * scale, cos, -sin)
    g_key = rotate(dot(g_scores, query, ((0,), (0,))) * scale, cos, -sin)
    g_mixed = jnp.concatenate([g_query, g_key, g_value], axis=1).astype(BF)
    grad_qkv = dot(h1, g_mixed, ((0,), (0,))).astype(BF)
    grad_qkv_bias = jnp.sum(g_mixed.astype(F32), axis=0)
    e1 = dot(g_mixed, w_qkv, ((1,), (1,)))
    e_part = (e1 * gain_one + e2 * gain_two).astype(BF)
    e_own = lax.psum_scatter(e_part, CHIPS, scatter_dimension=0, tiled=True).astype(F32)
    center_own = x_rows - jnp.mean(x_rows, axis=-1, keepdims=True)
    rstd_own = lax.rsqrt(jnp.mean(center_own * center_own, axis=-1, keepdims=True) + NORM_EPS)
    xhat_own = center_own * rstd_own
    grad_x = rstd_own * (
        e_own - jnp.mean(e_own, axis=-1, keepdims=True) - xhat_own * jnp.mean(e_own * xhat_own, axis=-1, keepdims=True)
    )
    input_grad = move((g_own.astype(F32) + grad_x).astype(BF), BACK)

    def at_chip(vec, parts):
        full = jnp.zeros((parts, 8, vec.shape[0] // parts), F32)
        return lax.dynamic_update_slice_in_dim(full, vec.reshape(parts, 1, -1), chip, 1).reshape(-1)

    norms = [
        jnp.sum(e1 * xhat, axis=0), jnp.sum(e1, axis=0), jnp.sum(e2 * xhat, axis=0), jnp.sum(e2, axis=0),
        jnp.sum(g_own.astype(F32), axis=0),
    ]
    sums = jnp.concatenate(norms + [at_chip(grad_qkv_bias, 3), at_chip(grad_up_bias, 1)])
    sums = lax.psum(sums, ("x", "y", "c", "w", "z"))
    owner = chip * 2 + core

    def own_part(start, size):
        step = size // 16
        return lax.dynamic_slice_in_dim(sums, start + owner * step, step)

    grad_g1, grad_b1, grad_g2, grad_b2, grad_ob = (own_part(i * width, width) for i in range(5))
    grad_qb = own_part(5 * width, 3 * width)
    grad_ub = own_part(8 * width, ff)

    down_own = core_sum(grad_rows[:ff_part].reshape(2, ff_part // 2, width), core, 0)
    out_own = core_sum(grad_rows[ff_part:].reshape(2, head_dim // 2, width), core, 0)
    grad_down, grad_out = lax.psum((down_own, out_own), COPIES)

    def by_columns(grad):
        cols = grad.shape[1]
        own = core_sum(grad.reshape(8, 2, rows, cols), core, 1)
        own = own.transpose(1, 0, 2)
        own = lax.psum_scatter(own, COPIES, scatter_dimension=0, tiled=True)
        own = lax.all_to_all(own, CHIPS, 1, 1, tiled=True)
        return lax.all_gather(own, COPIES, axis=0, tiled=True)

    grad_up = by_columns(grad_up).reshape(rows, ff)
    grad_qkv = by_columns(grad_qkv).reshape(rows, HEADS, 3, head_dim).transpose(0, 2, 1, 3).reshape(rows, 3 * width)

    return (
        layer_output[None], input_grad[None], grad_g1, grad_b1, grad_qkv.astype(F32), grad_qb, grad_out.astype(F32),
        grad_ob, grad_g2, grad_b2, grad_up.astype(F32), grad_ub, grad_down.astype(F32), grad_ob,
    )


def solution(mesh):
    fine = Mesh(mesh.devices.reshape(2, 4, 2, 2, 4), ("x", "y", "c", "w", "z"))
    by_owner, by_place = ("x", "y", "c"), ("w", "z")
    act, vec, mat = P(by_owner, by_place, None), P(by_owner), P(by_owner, None)
    return jax.shard_map(
        body,
        mesh=fine,
        in_specs=(act, mat, act, vec, vec, mat, vec, mat, vec, vec, vec, mat, vec, mat, vec),
        out_specs=(act, act, vec, vec, mat, vec, mat, vec, vec, vec, mat, vec, mat, vec),
        check_vma=False,
    )
```

```python
import math

import jax
import jax.numpy as jnp
from jax import lax
from jax.experimental import pallas as pl
from jax.experimental.pallas import tpu as pltpu
from jax.sharding import Mesh, PartitionSpec as P

HEADS = 8
ROTARY = 64
NORM_EPS = 1e-05
MASKED = -1e30
BF = jnp.bfloat16
F32 = jnp.float32
LANES = 128
TILE = 256
VMEM_BYTES = 56 * 1024 * 1024
AXES = ("x", "y", "c", "w", "z")
SIZES = {"x": 2, "y": 4, "c": 2, "w": 2, "z": 4}
CHIPS = ("x", "y")


def pairs_of(axes, target):
    pairs = []
    total = math.prod(SIZES[a] for a in axes)
    for source in range(total):
        rest, at = source, {}
        for a in reversed(axes):
            at[a] = rest % SIZES[a]
            rest //= SIZES[a]
        to, number = {**at, **target(at)}, 0
        for a in axes:
            number = number * SIZES[a] + to[a] % SIZES[a]
        pairs.append((source, number))
    return pairs


def send(block, axes, target):
    return lax.ppermute(block, axes, pairs_of(axes, target))


def place_target(at):
    if at["c"] == 0:
        return {"x": at["w"], "y": at["y"] + at["z"], "w": at["x"], "z": at["y"]}
    return {"x": at["x"] ^ at["w"], "y": at["y"] + at["z"], "z": at["y"]}


MOVES = pairs_of(AXES, place_target)


def move(block):
    return lax.ppermute(block, AXES, MOVES)


def move_back(block):
    return lax.ppermute(block, AXES, [(b, a) for a, b in MOVES])


def swap_core(block):
    return send(block, ("c",), lambda at: {"c": at["c"] ^ 1})


def swap_x(block):
    return send(block, ("x", "c", "w"), lambda at: {"x": at["x"] ^ 1, "w": at["w"] ^ at["c"]})


def swap_w(block):
    return send(block, ("w",), lambda at: {"w": at["w"] ^ 1})


def ring(block, axis, step):
    return send(block, (axis,), lambda at: {axis: at[axis] + step})


def add(*terms):
    return sum(t.astype(F32) for t in terms)


def mark(array):
    return array[(0,) * array.ndim]


def tie(block, after):
    return block + (after * 0).astype(block.dtype)


def gather(block, after=(None, None, None)):
    n = block.shape[0] // 2
    with jax.named_scope("ring"):
        above, below = ring(block, "y", -1), ring(block, "y", 1)
    with jax.named_scope("own_x"):
        own_x = swap_x(block)
    near = jnp.concatenate([above, below], axis=0)
    near = near if after[0] is None else tie(near, after[0])
    with jax.named_scope("far"):
        far = jnp.concatenate([ring(near[n * 2 : n * 3], "y", 1), ring(near[n : 2 * n], "y", -1)], axis=0)
    far = far if after[1] is None else tie(far, after[1])
    with jax.named_scope("near_x"):
        near_x = swap_x(near)
    with jax.named_scope("far_x"):
        far_x = swap_x(far)
    far_x = far_x if after[2] is None else tie(far_x, after[2])
    return [block, near, far, own_x, near_x, far_x]


def scatter_x(part, after=None):
    later = [] if after is None else [after * 0]
    with jax.named_scope("far_x"):
        far = add(part[3], swap_x(part[7]), *later).astype(BF)
    with jax.named_scope("near_x"):
        near = add(part[1:3], swap_x(part[5:7]), *later)
    with jax.named_scope("own_x"):
        own = add(part[0], swap_x(part[4]), *later)
    return far, near, own


def scatter_far(far, near, after=None):
    m = far.shape[0] // 2
    if after is not None:
        near = tie(near, after)
    with jax.named_scope("far"):
        above = jnp.concatenate([near[0, :m] + ring(far[:m], "y", 1).astype(F32), near[0, m:]], axis=0).astype(BF)
        below = jnp.concatenate([near[1, :m], near[1, m:] + ring(far[m:], "y", -1).astype(F32)], axis=0).astype(BF)
    return above, below


def scatter_near(above, below, own, after=None):
    later = [] if after is None else [after * 0]
    with jax.named_scope("ring"):
        return add(own, ring(above, "y", 1), ring(below, "y", -1), *later)


def mm(a, b, ca=1, cb=0):
    return lax.dot_general(a, b, (((ca,), (cb,)), ((), ())), preferred_element_type=F32)


def turn(head, table, back):
    first = head[:, :LANES]
    n = LANES
    left = pltpu.roll(first, n - 32, 1)
    right = pltpu.roll(first, 32, 1)
    sines = left * table[:, n : 2 * n] + right * table[:, 2 * n :]
    first = first * table[:, :n] + (-sines if back else sines)
    return jnp.concatenate([first, head[:, LANES:]], axis=1)


def whole(shape):
    return pl.BlockSpec(shape, lambda *_: (0,) * len(shape), pipeline_mode=pl.Buffered(1))


def kept(shape):
    return pl.BlockSpec(shape, lambda *_: (0,) * len(shape))


def tiles(*shape, axis=0):
    return pl.BlockSpec(shape, lambda i: tuple(i if a == axis else 0 for a in range(len(shape))))


def anywhere(count):
    return [pl.BlockSpec(memory_space=pl.ANY)] * count


def params():
    return pltpu.CompilerParams(vmem_limit_bytes=VMEM_BYTES, dimension_semantics=("arbitrary",))


def project_kernel(where, x, weights, table, h1, h2, qkv, act, slope, norm, b_sum, cols, small, bias_q, bias_u, sem):
    chip = where[0]
    first = pl.program_id(0) == 0

    @pl.when(first)
    def _():
        pltpu.make_async_copy(weights, cols, sem).start()

    v = x[...].astype(F32)
    center = v - jnp.mean(v, axis=-1, keepdims=True)
    rstd = lax.rsqrt(jnp.mean(center * center, axis=-1, keepdims=True) + NORM_EPS)
    xhat = center * rstd
    q3, half, width = qkv.shape[1], act.shape[2], x.shape[1]
    dim = q3 // 3

    @pl.when(first)
    def _():
        pltpu.make_async_copy(weights, cols, sem).wait()
        for f in range(16):
            small[f] = cols[f % 2, 0, f // 2, :16, q3 + 2 * half :].astype(F32)
            at = slice(f * LANES, (f + 1) * LANES)
            for k, row in enumerate((0, 1, 3, 4)):
                norm[k : k + 1, at] = small[f, row : row + 1]
            b_sum[:, at] = small[f, 2:3] + small[f, 5:6]
        for k in range(6):
            block = (k // 2) * 16 + chip * 2 + k % 2
            bias_q[:, k * LANES : (k + 1) * LANES] = small[lax.div(block, 3), pl.ds(6 + lax.rem(block, 3), 1), :]
        for k in range(8):
            bias_u[:, k * LANES : (k + 1) * LANES] = small[chip * 2 + k // 4, 9 + k % 4 : 10 + k % 4]

    one = (xhat * norm[0:1] + norm[1:2]).astype(BF)
    two = (xhat * norm[2:3] + norm[3:4]).astype(BF)
    h1[...] = one
    h2[...] = two
    step = cols.shape[3]
    mixed = jnp.broadcast_to(bias_q[...], (v.shape[0], q3))
    for h in range(8):
        mixed += mm(one[:, h * 256 : (h + 1) * 256], cols[:, :, h, :, :q3].reshape(8 * step, -1))
    qkv[:, :dim] = turn(mixed[:, :dim], table[...], False).astype(BF)
    qkv[:, dim : 2 * dim] = turn(mixed[:, dim : 2 * dim], table[...], False).astype(BF)
    qkv[:, 2 * dim :] = mixed[:, 2 * dim :].astype(BF)
    for part in range(2):
        pre = jnp.broadcast_to(bias_u[:, part * half : (part + 1) * half], (v.shape[0], half))
        start = q3 + part * half
        for h in range(8):
            pre += mm(two[:, h * 256 : (h + 1) * 256], cols[:, :, h, :, start : start + half].reshape(8 * step, -1))
        phi = 0.5 * (1.0 + lax.erf(pre * 0.7071067811865476))
        act[part] = (pre * phi).astype(BF)
        slope[part] = (phi + pre * jnp.exp(-0.5 * pre * pre) * 0.3989422804014327).astype(BF)


def project(where, x, weights, table, q3, ff):
    n, width = x.shape

    def rows(*shape, axis=0):
        return pl.BlockSpec(shape, lambda i, s: tuple(i if a == axis else 0 for a in range(len(shape))))

    return pl.pallas_call(
        project_kernel,
        grid_spec=pltpu.PrefetchScalarGridSpec(
            num_scalar_prefetch=1,
            grid=(n // TILE,),
            in_specs=[rows(TILE, width), *anywhere(1), rows(TILE, 3 * LANES)],
            out_specs=[
                rows(TILE, width), rows(TILE, width), rows(TILE, q3), rows(2, TILE, ff // 2, axis=1),
                rows(2, TILE, ff // 2, axis=1), kept((4, width)), kept((1, width)),
            ],
            scratch_shapes=[
                pltpu.VMEM(weights.shape, BF), pltpu.VMEM((16, 16, LANES), F32), pltpu.VMEM((1, q3), F32),
                pltpu.VMEM((1, ff), F32), pltpu.SemaphoreType.DMA,
            ],
        ),
        out_shape=[
            jax.ShapeDtypeStruct((n, width), BF), jax.ShapeDtypeStruct((n, width), BF), jax.ShapeDtypeStruct((n, q3), BF),
            jax.ShapeDtypeStruct((2, n, ff // 2), BF), jax.ShapeDtypeStruct((2, n, ff // 2), BF),
            jax.ShapeDtypeStruct((4, width), F32), jax.ShapeDtypeStruct((1, width), F32),
        ],
        compiler_params=params(),
        cost_estimate=pl.CostEstimate(flops=2 * n * width * (q3 + ff), bytes_accessed=30 << 20, transcendentals=2 * n * ff),
        name="project",
    )(where, x, weights, table)


def attend_kernel(q, kv, place_q, place_k, doc_q, doc_k, prob, att):
    dim = kv.shape[1] // 3
    key, value = kv[:, dim : 2 * dim], kv[:, 2 * dim :]
    scores = mm(q[:, :dim], key, 1, 1) * (dim ** -0.5)
    pq, pk = place_q[...], place_k[...]
    allowed = ((doc_q[...] == doc_k[...]) & (pk <= pq)) | (pk == pq)
    scores = jnp.where(allowed, scores, MASKED)
    expo = jnp.exp(scores - jnp.max(scores, axis=-1, keepdims=True))
    p = (expo * (1.0 / jnp.sum(expo, axis=-1, keepdims=True))).astype(BF)
    prob[...] = p
    out = mm(p, value).astype(BF)
    att[0] = out[:, : dim // 2]
    att[1] = out[:, dim // 2 :]


def attend(qkv, places, docs):
    n, q3 = qkv.shape
    dim = q3 // 3
    doc_k = jnp.where(docs < 0, -2, docs)
    return pl.pallas_call(
        attend_kernel,
        grid=(n // TILE,),
        in_specs=[tiles(TILE, q3), whole((n, q3)), tiles(TILE, 1), whole((1, n)), tiles(TILE, 1), whole((1, n))],
        out_specs=[tiles(TILE, n), tiles(2, TILE, dim // 2, axis=1)],
        out_shape=[jax.ShapeDtypeStruct((n, n), BF), jax.ShapeDtypeStruct((2, n, dim // 2), BF)],
        compiler_params=params(),
        cost_estimate=pl.CostEstimate(flops=4 * n * n * dim, bytes_accessed=5 << 20, transcendentals=n * n),
        name="attend",
    )(qkv, qkv, places[:, None], places[None], docs[:, None], doc_k[None])


def attend_back_kernel(q, kv, prob, g, table_q, table, *rest):
    out, key_sum, value_sum = rest[-3:]
    i = pl.program_id(0)
    n = kv.shape[0]
    dim = kv.shape[1] // 3
    key, value = kv[:, dim : 2 * dim], kv[:, 2 * dim :]
    g_tile = jnp.concatenate([g[0], g[1]], axis=1)
    p_low = prob[...]
    p = p_low.astype(F32)
    g_prob = mm(g_tile, value, 1, 1)
    inner = jnp.sum(p * g_prob, axis=-1, keepdims=True)
    g_scores = (p * (g_prob - inner)).astype(BF)
    scale = dim ** -0.5
    g_query = mm(g_scores, key) * scale
    out[pl.ds(i * TILE, TILE), :dim] = turn(g_query, table_q[...], True).astype(BF)
    g_key = mm(g_scores, q[:, :dim], 0, 0)
    g_value = mm(p_low, g_tile, 0, 0)

    @pl.when(i == 0)
    def _():
        key_sum[...] = g_key
        value_sum[...] = g_value

    @pl.when(i > 0)
    def _():
        key_sum[...] += g_key
        value_sum[...] += g_value

    @pl.when(i == pl.num_programs(0) - 1)
    def _():
        out[:, dim : 2 * dim] = turn(key_sum[...] * scale, table[...], True).astype(BF)
        out[:, 2 * dim :] = value_sum[...].astype(BF)


def attend_back(qkv, prob, g_att, table, after):
    n, q3 = qkv.shape
    dim = q3 // 3
    return pl.pallas_call(
        attend_back_kernel,
        grid=(n // TILE,),
        in_specs=[
            tiles(TILE, q3), whole((n, q3)), tiles(TILE, n), tiles(2, TILE, dim // 2, axis=1), tiles(TILE, 3 * LANES),
            whole((n, 3 * LANES)), *anywhere(len(after)),
        ],
        out_specs=kept((n, q3)),
        out_shape=jax.ShapeDtypeStruct((n, q3), BF),
        scratch_shapes=[pltpu.VMEM((n, dim), F32), pltpu.VMEM((n, dim), F32)],
        compiler_params=params(),
        cost_estimate=pl.CostEstimate(flops=8 * n * n * dim, bytes_accessed=8 << 20, transcendentals=0),
        name="attend_back",
    )(qkv, qkv, prob, g_att, table, table, *after)


def branch_grad_kernel(core, g, mine, twin, slope, *rest):
    g_pre, g_att, bias = rest[-3:]
    c = core[0]
    half = slope.shape[2]
    own = mm(g[...], mine[...], 1, 1)
    other = mm(g[...], twin[...], 1, 1)

    @pl.when(pl.program_id(0) == 0)
    def _():
        bias[...] = jnp.zeros_like(bias)

    for at, part in ((c, own), (1 - c, other)):
        pre = (part[:, :half] * slope[at].astype(F32)).astype(BF)
        g_pre[at] = pre
        g_att[at] = part[:, half:].astype(BF)
        bias[at] += jnp.sum(pre.astype(F32), axis=0, keepdims=True)


def branch_grad(core, g, mine, twin, slope, after):
    n, width = g.shape
    half = slope.shape[2]
    tail = mine.shape[0] - half
    return pl.pallas_call(
        branch_grad_kernel,
        grid_spec=pltpu.PrefetchScalarGridSpec(
            num_scalar_prefetch=1,
            grid=(n // TILE,),
            in_specs=[
                pl.BlockSpec((TILE, width), lambda i, s: (i, 0)), whole(mine.shape), whole(twin.shape),
                pl.BlockSpec((2, TILE, half), lambda i, s: (0, i, 0)), *anywhere(len(after)),
            ],
            out_specs=[
                pl.BlockSpec((2, TILE, half), lambda i, s: (0, i, 0)),
                pl.BlockSpec((2, TILE, tail), lambda i, s: (0, i, 0)), kept((2, 1, half)),
            ],
        ),
        out_shape=[
            jax.ShapeDtypeStruct((2, n, half), BF), jax.ShapeDtypeStruct((2, n, tail), BF),
            jax.ShapeDtypeStruct((2, 1, half), F32),
        ],
        compiler_params=params(),
        cost_estimate=pl.CostEstimate(flops=4 * n * width * (half + tail), bytes_accessed=16 << 20, transcendentals=0),
        name="branch_grad",
    )(core, g, mine, twin, slope, *after)


def branches_kernel(core, act, att, mine, twin, out):
    c = core[0]
    half = act.shape[2]
    own, other = (jnp.concatenate([act[k], att[k]], axis=1) for k in (c, 1 - c))
    total = mm(own, mine[...]) + mm(other, twin[...])
    out[...] = total.astype(BF).reshape(out.shape)


def branches_out(core, act, att, mine, twin):
    half, tail = act.shape[2], att.shape[2]
    n, width = act.shape[1], mine.shape[1]
    return pl.pallas_call(
        branches_kernel,
        grid_spec=pltpu.PrefetchScalarGridSpec(
            num_scalar_prefetch=1,
            grid=(n // TILE,),
            in_specs=[
                pl.BlockSpec((2, TILE, half), lambda i, s: (0, i, 0)), pl.BlockSpec((2, TILE, tail), lambda i, s: (0, i, 0)),
                whole(mine.shape), whole(twin.shape),
            ],
            out_specs=pl.BlockSpec((TILE // 128, 128, width), lambda i, s: (i, 0, 0)),
        ),
        out_shape=jax.ShapeDtypeStruct((n // 128, 128, width), BF),
        compiler_params=params(),
        cost_estimate=pl.CostEstimate(flops=4 * n * width * (half + tail), bytes_accessed=14 << 20, transcendentals=0),
        name="branches",
    )(core, act, att, mine, twin)


def partials_kernel(where, x, norm, g_mixed, g_pre, u_bias, dy_sum, weights, *rest):
    part, cols, sums, bias, sem = rest[-5:]
    chip = where[0]
    first = pl.program_id(0) == 0

    @pl.when(first)
    def _():
        pltpu.make_async_copy(weights, cols, sem).start()
        sums[...] = jnp.zeros_like(sums)
        bias[...] = jnp.zeros_like(bias)

    v = x[...].astype(F32)
    center = v - jnp.mean(v, axis=-1, keepdims=True)
    rstd = lax.rsqrt(jnp.mean(center * center, axis=-1, keepdims=True) + NORM_EPS)
    xhat = center * rstd
    step = cols.shape[3]
    half, q3 = g_pre.shape[2], g_mixed.shape[1]
    gm = g_mixed[...]
    gm_sum = jnp.sum(gm.astype(F32), axis=0, keepdims=True)
    for k in range(6):
        bias[k : k + 1] += gm_sum[:, k * LANES : (k + 1) * LANES]

    @pl.when(first)
    def _():
        pltpu.make_async_copy(weights, cols, sem).wait()

    n = 128
    slots = v.shape[0] // n
    i = pl.program_id(0)
    for h in range(8):
        at = slice(h * 256, (h + 1) * 256)
        wide = cols[:, :, h].reshape(8 * step, -1)
        one = mm(gm, wide[:, :q3], 1, 1)
        two = mm(g_pre[0], wide[:, q3 : q3 + half], 1, 1) + mm(g_pre[1], wide[:, q3 + half : q3 + 2 * half], 1, 1)
        e = (one * norm[0:1, at] + two * norm[2:3, at]).astype(BF)
        for s in range(slots):
            part[i * slots + s, :n, at] = e[s * n : (s + 1) * n]
        xh = xhat[:, at]
        sums[h, 0:1] += jnp.sum(one * xh, axis=0, keepdims=True)
        sums[h, 1:2] += jnp.sum(one, axis=0, keepdims=True)
        sums[h, 2:3] += jnp.sum(two * xh, axis=0, keepdims=True)
        sums[h, 3:4] += jnp.sum(two, axis=0, keepdims=True)

    @pl.when(i == pl.num_programs(0) - 1)
    def _():
        more = part.shape[1] - n
        for slot in range(8):
            to = where[2 + slot]
            row = [sums[to, k : k + 1] for k in range(4)] + [dy_sum[to]]
            for j in range(6):
                block = to * 6 + j
                section, rest_of = lax.div(block, 16), lax.rem(block, 16)
                value = bias[pl.ds(section * 2 + lax.rem(rest_of, 2), 1), :]
                row.append(jnp.where(lax.div(rest_of, 2) == chip, value, 0.0))
            row = jnp.concatenate(row, axis=1)
            if slot == 0:
                other = jnp.concatenate([u_bias[0], u_bias[1], jnp.zeros((1, row.shape[1] - 2 * half), F32)], axis=1)
            else:
                other = jnp.zeros_like(row)
            block = jnp.concatenate([row, other, jnp.zeros((more - 2, row.shape[1]), F32)], axis=0)
            part[slot, n:, :] = block.astype(BF)


def partials(where, x, norm, g_mixed, g_pre, u_bias, dy_sum, weights, after):
    n, width = x.shape
    half, q3 = g_pre.shape[2], g_mixed.shape[1]

    def rows(*shape, axis=0):
        return pl.BlockSpec(shape, lambda i, s: tuple(i if a == axis else 0 for a in range(len(shape))))

    return pl.pallas_call(
        partials_kernel,
        grid_spec=pltpu.PrefetchScalarGridSpec(
            num_scalar_prefetch=1,
            grid=(n // TILE,),
            in_specs=[
                rows(TILE, width), whole(norm.shape), rows(TILE, q3), rows(2, TILE, half, axis=1), whole(u_bias.shape),
                whole(dy_sum.shape), *anywhere(1 + len(after)),
            ],
            out_specs=kept((n // 128, 144, width)),
            scratch_shapes=[
                pltpu.VMEM(weights.shape, BF), pltpu.VMEM((8, 8, 256), F32), pltpu.VMEM((8, LANES), F32),
                pltpu.SemaphoreType.DMA,
            ],
        ),
        out_shape=jax.ShapeDtypeStruct((n // 128, 144, width), BF),
        compiler_params=params(),
        cost_estimate=pl.CostEstimate(flops=2 * n * width * (q3 + 2 * half), bytes_accessed=24 << 20, transcendentals=0),
        name="partials",
    )(where, x, norm, g_mixed, g_pre, u_bias, dy_sum, weights, *after)


def half_grad_kernel(core, left, right, *rest):
    keep, give, pair = rest[-3:]
    c = core[0]
    n = pair.shape[1]
    step = n // 4
    done = 0
    for part in range(right.shape[0]):
        res = mm(left[...], right[part], 0, 0).astype(BF)
        w = res.shape[1]
        pair[0, :, done : done + w] = res[:n]
        pair[1, :, done : done + w] = res[n:]
        done += w
    for z in range(4):
        at = slice(z * step, (z + 1) * step)
        keep[z, 0] = pair[c, at]
        give[z, 0] = pair[1 - c, at]


def half_grad(core, left, right, after):
    n, width = left.shape
    cols = right.shape[2] * right.shape[0]
    rows = width // 16
    return pl.pallas_call(
        half_grad_kernel,
        grid_spec=pltpu.PrefetchScalarGridSpec(
            num_scalar_prefetch=1,
            grid=(8,),
            in_specs=[pl.BlockSpec((n, 2 * rows), lambda i, s: (0, i)), whole(right.shape), *anywhere(len(after))],
            out_specs=[pl.BlockSpec((4, 1, rows // 4, cols), lambda i, s: (0, i, 0, 0))] * 2,
            scratch_shapes=[pltpu.VMEM((2, rows, cols), BF)],
        ),
        out_shape=[jax.ShapeDtypeStruct((4, 8, rows // 4, cols), BF)] * 2,
        compiler_params=params(),
        cost_estimate=pl.CostEstimate(flops=2 * n * width * cols, bytes_accessed=12 << 20, transcendentals=0),
        name="half_grad",
    )(core, left, right, *after)


def rows_grad_kernel(core, act, att, g, *rest):
    keep, give = rest[-2:]
    whole_g = g[...]
    act_t = mm(act[0], whole_g, 0, 0).astype(BF)
    att_t = mm(att[0], whole_g, 0, 0).astype(BF)
    a, b = act_t.shape[0] // 8, att_t.shape[0] // 8
    for p, out in enumerate((give, keep)):
        @pl.when(pl.program_id(0) == p)
        def _():
            for i in range(8):
                out[i // 4, i % 4, :a] = act_t[i * a : (i + 1) * a]
                out[i // 4, i % 4, a:] = att_t[i * b : (i + 1) * b]


def rows_grad(core, act, att, g, after):
    n, width = g.shape
    half, tail = act.shape[2], att.shape[2]
    shape = (2, 4, (half + tail) // 8, width)
    return pl.pallas_call(
        rows_grad_kernel,
        grid_spec=pltpu.PrefetchScalarGridSpec(
            num_scalar_prefetch=1,
            grid=(2,),
            in_specs=[
                pl.BlockSpec((1, n, half), lambda p, s: (s[0] * p + (1 - s[0]) * (1 - p), 0, 0)),
                pl.BlockSpec((1, n, tail), lambda p, s: (s[0] * p + (1 - s[0]) * (1 - p), 0, 0)), whole(g.shape),
                *anywhere(len(after)),
            ],
            out_specs=[kept(shape), kept(shape)],
        ),
        out_shape=[jax.ShapeDtypeStruct(shape, BF)] * 2,
        compiler_params=params(),
        cost_estimate=pl.CostEstimate(flops=4 * n * width * (half + tail), bytes_accessed=14 << 20, transcendentals=0),
        name="rows_grad",
    )(core, act, att, g, *after)


def columns_out_kernel(where, *refs):
    blocks, (qkv, up) = refs[:4], refs[4:]
    a, w = pl.program_id(0), pl.program_id(1)
    offset = lax.rem(where[0] - a + 4, 4)
    at = jnp.where(w == where[1], 0, 1)
    dim, part = qkv.shape[1] // 24, up.shape[1] // 8
    for k, b in enumerate(blocks):
        @pl.when(offset == k)
        def _():
            for h in range(8):
                for s in range(3):
                    to = (s * 8 + h) * dim
                    qkv[:, to : to + dim] = b[at, h, :, s * dim : (s + 1) * dim].astype(F32)
                up[:, h * part : (h + 1) * part] = b[at, h, :, 3 * dim :].astype(F32)


def columns_out(where, blocks, q3, ff):
    rows = blocks[0].shape[2]
    return pl.pallas_call(
        columns_out_kernel,
        grid_spec=pltpu.PrefetchScalarGridSpec(
            num_scalar_prefetch=1,
            grid=(4, 2),
            in_specs=[whole(b.shape) for b in blocks],
            out_specs=[pl.BlockSpec((rows, n), lambda a, w, s: (a * 2 + w, 0)) for n in (8 * q3, 8 * ff)],
        ),
        out_shape=[jax.ShapeDtypeStruct((8 * rows, n), F32) for n in (8 * q3, 8 * ff)],
        compiler_params=pltpu.CompilerParams(vmem_limit_bytes=VMEM_BYTES),
        cost_estimate=pl.CostEstimate(flops=0, bytes_accessed=12 << 20, transcendentals=0),
        name="columns_out",
    )(where, *blocks)


def rows_out_kernel(where, mine, twin, down, out):
    w, a = pl.program_id(0), pl.program_id(1)
    offset = lax.rem(where[0] - a + 4, 4)
    n = down.shape[0]
    for k, b in enumerate((mine, twin)):
        @pl.when((w == where[1]) == (k == 0))
        def _():
            v = b[offset]
            down[...] = v[:n].astype(F32)
            out[...] = v[n:].astype(F32)


def rows_out(where, mine, twin):
    _, n, width = mine.shape
    cut = n * 4 // 5
    return pl.pallas_call(
        rows_out_kernel,
        grid_spec=pltpu.PrefetchScalarGridSpec(
            num_scalar_prefetch=1,
            grid=(2, 4),
            in_specs=[whole(mine.shape), whole(twin.shape)],
            out_specs=[
                pl.BlockSpec((cut, width), lambda w, a, s: (w * 4 + a, 0)),
                pl.BlockSpec((n - cut, width), lambda w, a, s: (w * 4 + a, 0)),
            ],
        ),
        out_shape=[jax.ShapeDtypeStruct((8 * cut, width), F32), jax.ShapeDtypeStruct((8 * (n - cut), width), F32)],
        compiler_params=pltpu.CompilerParams(vmem_limit_bytes=VMEM_BYTES),
        cost_estimate=pl.CostEstimate(flops=0, bytes_accessed=8 << 20, transcendentals=0),
        name="rows_out",
    )(where, mine, twin)


def small_out_kernel(where, total, norms, q_bias, u_bias):
    core = where[1]
    for k in range(5):
        pair = [total[0:1, (2 * k + c) * LANES : (2 * k + c + 1) * LANES] for c in range(2)]
        norms[k : k + 1] = jnp.where(core == 0, pair[0], pair[1])
    for j in range(3):
        pair = [total[0:1, (10 + 3 * c + j) * LANES : (11 + 3 * c + j) * LANES] for c in range(2)]
        q_bias[j : j + 1] = jnp.where(core == 0, pair[0], pair[1])
    for j in range(4):
        pair = [total[1:2, (4 * c + j) * LANES : (4 * c + j + 1) * LANES] for c in range(2)]
        u_bias[j : j + 1] = jnp.where(core == 0, pair[0], pair[1])


def small_out(where, total):
    return pl.pallas_call(
        small_out_kernel,
        in_specs=[pl.BlockSpec(memory_space=pltpu.SMEM), pl.BlockSpec(memory_space=pltpu.VMEM)],
        out_specs=[pl.BlockSpec(memory_space=pltpu.VMEM)] * 3,
        out_shape=[jax.ShapeDtypeStruct((n, LANES), F32) for n in (5, 3, 4)],
        name="small_out",
    )(where, total)


def pair_sum(keep, give, swap, after=None):
    later = [] if after is None else [after * 0]
    return add(keep, swap(give), *later).astype(BF)


def copies_scatter(pieces, after=None):
    z = lax.axis_index("z")
    later = [] if after is None else [after * 0]

    def piece(offset):
        return lax.dynamic_index_in_dim(pieces, (z + offset) % 4, 0, keepdims=False)

    return add(piece(0), *(ring(piece(o), "z", o) for o in (1, 2, 3)), *later)


def copies_gather(piece):
    return [piece] + [ring(piece, "z", o) for o in (1, 2, 3)]


def body(
    tokens, segment_ids, out_cotangent, ln1_gain, ln1_bias, qkv_weight, qkv_bias, out_weight, out_bias,
    ln2_gain, ln2_bias, up_weight, up_bias, down_weight, down_bias,
):
    _, shard, width = tokens.shape
    head_dim = width // HEADS
    ff = up_weight.shape[1]
    ff_part = ff // 8
    rows = qkv_weight.shape[0]
    x, y, core, w, z = (lax.axis_index(a) for a in AXES)
    chip = x * 4 + y
    core_at = core.astype(jnp.int32).reshape(1)
    copy_at = jnp.stack([z, w]).astype(jnp.int32)
    chip_at = jnp.stack([chip, core]).astype(jnp.int32)

    with jax.named_scope("x"):
        x_own = move(tokens[0])
        x_parts = gather(x_own)
    with jax.named_scope("ids"):
        ids = move(segment_ids)[0]
    x_all = jnp.concatenate(x_parts, axis=0)
    with jax.named_scope("dy"):
        g_own = move(tie(out_cotangent[0], x_own[0, 0]))

    step = rows // 4
    q_part, u_part = (lax.dynamic_slice_in_dim(m, z * step, step, 0) for m in (qkv_weight, up_weight))
    q_part = q_part.reshape(step, 3, 8, head_dim).transpose(2, 0, 1, 3).reshape(8, step, 3 * head_dim)
    u_part = u_part.reshape(step, 8, ff_part).transpose(1, 0, 2)
    small = jnp.concatenate([ln1_gain, ln1_bias, out_bias, ln2_gain, ln2_bias, down_bias, qkv_bias, up_bias])
    n_small = small.shape[0] // LANES
    small = jnp.pad(small.reshape(n_small, LANES), ((0, step - n_small), (0, 0)))
    cols = jnp.concatenate([q_part, u_part, jnp.broadcast_to(small[None], (8, step, LANES))], axis=2)
    with jax.named_scope("weights"):
        cols = lax.all_to_all(cols, CHIPS, 0, 0, tiled=True)
        cols = lax.all_gather(tie(cols, mark(x_own)), ("c", "z"), axis=0).reshape(2, 4, *cols.shape)
    w_mine = jnp.concatenate([down_weight, out_weight], axis=0)
    with jax.named_scope("row_weights"):
        w_twin = swap_core(w_mine)

    y_offset = jnp.array([0, 1, 3, 2], jnp.int32)
    slot = jnp.arange(8, dtype=jnp.int32)
    slot_chip = (x ^ (slot // 4)) * 4 + (y + y_offset[slot % 4]) % 4
    slot_at = jnp.concatenate([chip_at, slot_chip.astype(jnp.int32)])
    group = w ^ (x & core)
    block = ((x ^ (group & core)) ^ (slot // 4)) * 4 + (y - z + y_offset[slot % 4] + 4) % 4
    places = (block[:, None] * shard + jnp.arange(shard, dtype=jnp.int32)[None, :]).reshape(8 * shard)
    half = ROTARY // 2
    lane = jnp.arange(LANES, dtype=jnp.int32)[None]
    freqs = jnp.exp((lane % half).astype(F32) * (-2.0 * math.log(10000.0) / ROTARY))
    angles = places.astype(F32)[:, None] * freqs
    sin = jnp.sin(angles)
    table = jnp.concatenate(
        [
            jnp.where(lane < ROTARY, jnp.cos(angles), 1.0), jnp.where(lane < half, -sin, 0.0),
            jnp.where((lane >= half) & (lane < ROTARY), sin, 0.0),
        ],
        axis=1,
    )
    docs = jnp.take(ids.reshape(8, shard), block, axis=0).reshape(8 * shard)

    h1, h2, qkv, act, slope, norm, b_sum = project(chip_at, x_all, cols, table, 3 * head_dim, ff_part)
    prob, attended = attend(qkv, places, docs)
    out_part = branches_out(core_at, act, attended, w_mine, w_twin)
    with jax.named_scope("dy"):
        g_parts = gather(tie(g_own, mark(x_parts[2])), (mark(qkv), mark(attended), mark(out_part)))
    g_all = jnp.concatenate(g_parts, axis=0)

    g_pre, g_att, up_bias_grad = branch_grad(core_at, g_all, w_mine, w_twin, slope, (out_part,))
    with jax.named_scope("out"):
        out_far, out_near, out_own = scatter_x(out_part, mark(up_bias_grad))
    rows_keep, rows_give = rows_grad(core_at, act, attended, g_all, (g_pre, out_far))
    with jax.named_scope("out"):
        out_above, out_below = scatter_far(out_far, out_near, mark(rows_give).astype(F32))
    g_mixed = attend_back(qkv, prob, g_att, table, (rows_give, out_above, out_below))
    with jax.named_scope("out"):
        out_sum = scatter_near(out_above, out_below, out_own, mark(g_mixed).astype(F32))
    with jax.named_scope("rows/core"):
        rows_part = pair_sum(rows_keep, rows_give, swap_core, mark(g_mixed).astype(F32))
    x_rows = x_own.astype(F32)
    layer_output = (x_rows + out_sum + b_sum).astype(BF)
    qkv_keep, qkv_give = half_grad(core_at, h1, g_mixed[None], (layer_output, rows_part))
    with jax.named_scope("out/back"):
        layer_output = move_back(layer_output)
    up_keep, up_give = half_grad(core_at, h2, g_pre, (qkv_give,))
    with jax.named_scope("rows/w"):
        rows_part = pair_sum(
            lax.dynamic_index_in_dim(rows_part, w, 0, keepdims=False),
            lax.dynamic_index_in_dim(rows_part, 1 - w, 0, keepdims=False), swap_w, mark(up_give).astype(F32),
        )
    with jax.named_scope("qkv/core"):
        qkv_part = pair_sum(qkv_keep, qkv_give, swap_core, mark(up_give).astype(F32))
    dy_sum = jnp.sum(g_own.astype(F32), axis=0).reshape(8, 1, 256)
    part = partials(slot_at, x_all, norm, g_mixed, g_pre, up_bias_grad, dy_sum, cols, (up_give, qkv_part, rows_part))
    last = mark(part).astype(F32)

    with jax.named_scope("up/core"):
        up_part = pair_sum(up_keep, up_give, swap_core, last)
    with jax.named_scope("rows/z"):
        rows_part = copies_scatter(rows_part, last).astype(BF)
    with jax.named_scope("qkv/z"):
        qkv_part = copies_scatter(qkv_part, last).astype(BF)
    with jax.named_scope("up/z"):
        up_part = copies_scatter(up_part).astype(BF)
    with jax.named_scope("rows/z_back"):
        rows_part = jnp.stack(copies_gather(rows_part))
    with jax.named_scope("rows/w_back"):
        rows_twin = swap_w(rows_part)
    grad_down, grad_out = rows_out(copy_at, rows_part, rows_twin)
    columns = jnp.concatenate([qkv_part, up_part], axis=2).reshape(8, 2, step // 2, -1)
    with jax.named_scope("columns/w"):
        piece = pair_sum(
            lax.dynamic_index_in_dim(columns, w, 1, keepdims=False),
            lax.dynamic_index_in_dim(columns, 1 - w, 1, keepdims=False), swap_w,
        )
    with jax.named_scope("columns/chips"):
        piece = lax.all_to_all(piece, CHIPS, 0, 0, tiled=True)
    with jax.named_scope("columns/w_back"):
        both = jnp.stack([piece, swap_w(piece)])
    with jax.named_scope("columns/z_back"):
        blocks = copies_gather(both)
    grad_qkv, grad_up = columns_out(copy_at, blocks, 3 * head_dim, ff_part)

    with jax.named_scope("part"):
        far, near, own = scatter_x(part)
        total = scatter_near(*scatter_far(far, near), own)
    center = x_rows - jnp.mean(x_rows, axis=-1, keepdims=True)
    rstd = lax.rsqrt(jnp.mean(center * center, axis=-1, keepdims=True) + NORM_EPS)
    xhat = center * rstd
    e = total[:shard]
    grad_x = rstd * (e - jnp.mean(e, axis=-1, keepdims=True) - xhat * jnp.mean(e * xhat, axis=-1, keepdims=True))
    input_grad = (g_own.astype(F32) + grad_x).astype(BF)
    with jax.named_scope("part/back"):
        input_grad = move_back(input_grad)

    sums = total[shard : shard + 2]
    with jax.named_scope("small/z"):
        sums = add(sums, ring(sums, "z", 1), ring(sums, "z", 2), ring(sums, "z", 3))
    with jax.named_scope("small/w"):
        sums = add(sums, swap_w(sums))
    with jax.named_scope("small/core"):
        sums = add(sums, swap_core(sums))
    norms, grad_qb, grad_ub = small_out(chip_at, sums)

    return (
        layer_output[None], input_grad[None], norms[0], norms[1], grad_qkv, grad_qb.reshape(-1), grad_out,
        norms[4], norms[2], norms[3], grad_up, grad_ub.reshape(-1), grad_down, norms[4],
    )


def solution(mesh):
    fine = Mesh(mesh.devices.reshape(*SIZES.values()), AXES)
    by_owner, by_place = ("x", "y", "c"), ("w", "z")
    act, vec, mat = P(by_owner, by_place, None), P(by_owner), P(by_owner, None)
    return jax.shard_map(
        body,
        mesh=fine,
        in_specs=(act, mat, act, vec, vec, mat, vec, mat, vec, vec, vec, mat, vec, mat, vec),
        out_specs=(act, act, vec, vec, mat, vec, mat, vec, vec, vec, mat, vec, mat, vec),
        check_vma=False,
    )
```

```python
import math

import jax
import jax.numpy as jnp
from jax import lax
from jax.experimental import pallas as pl
from jax.experimental.pallas import tpu as pltpu
from jax.sharding import Mesh, PartitionSpec as P

HEADS = 8
ROTARY = 64
NORM_EPS = 1e-05
MASKED = -1e30
BF = jnp.bfloat16
F32 = jnp.float32
LANES = 128
TILE = 256
VMEM_BYTES = 56 * 1024 * 1024
AXES = ("x", "y", "c", "w", "z")
SIZES = {"x": 2, "y": 4, "c": 2, "w": 2, "z": 4}
CHIPS = ("x", "y")


def pairs_of(axes, target):
    pairs = []
    total = math.prod(SIZES[a] for a in axes)
    for source in range(total):
        rest, at = source, {}
        for a in reversed(axes):
            at[a] = rest % SIZES[a]
            rest //= SIZES[a]
        to, number = {**at, **target(at)}, 0
        for a in axes:
            number = number * SIZES[a] + to[a] % SIZES[a]
        pairs.append((source, number))
    return pairs


def send(block, axes, target):
    return lax.ppermute(block, axes, pairs_of(axes, target))


def place_target(at):
    if at["c"] == 0:
        return {"x": at["w"], "y": at["y"] + at["z"], "w": at["x"], "z": at["y"]}
    return {"x": at["x"] ^ at["w"], "y": at["y"] + at["z"], "z": at["y"]}


MOVES = pairs_of(AXES, place_target)


def move(block):
    return lax.ppermute(block, AXES, MOVES)


def move_back(block):
    return lax.ppermute(block, AXES, [(b, a) for a, b in MOVES])


def swap_core(block):
    return send(block, ("c",), lambda at: {"c": at["c"] ^ 1})


def swap_x(block):
    return send(block, ("x", "c", "w"), lambda at: {"x": at["x"] ^ 1, "w": at["w"] ^ at["c"]})


def swap_w(block):
    return send(block, ("w",), lambda at: {"w": at["w"] ^ 1})


def ring(block, axis, step):
    return send(block, (axis,), lambda at: {axis: at[axis] + step})


def add(*terms):
    return sum(t.astype(F32) for t in terms)


def gather(where, block):
    n = block.shape[0] // 2
    with jax.named_scope("own_x"):
        own_x = swap_x(block)
    with jax.named_scope("ring"):
        above, below = ring(block, "y", -1), ring(block, "y", 1)
    above, below = pinned(where, [above, below], (own_x,))
    with jax.named_scope("far"):
        far = [ring(below[:n], "y", 1), ring(above[n:], "y", -1)]
    with jax.named_scope("near_x"):
        near_x = [swap_x(above), swap_x(below)]
    far = jnp.concatenate(far, axis=0)
    with jax.named_scope("far_x"):
        far_x = swap_x(far)
    return [above, below, block, far, *near_x, own_x, far_x]


def gather_line(block):
    with jax.named_scope("ring"):
        return [ring(block, "y", -1), ring(block, "y", 1), block, ring(block, "y", 2)]


def scatter(part):
    with jax.named_scope("far_x"):
        far = add(part[3], swap_x(part[7])).astype(BF)
    with jax.named_scope("near_x"):
        rest = add(part[:3], swap_x(part[4:7]))
    near, own = rest[:2], rest[2]
    m = far.shape[0] // 2
    with jax.named_scope("far"):
        above = jnp.concatenate([near[0, :m] + ring(far[:m], "y", 1).astype(F32), near[0, m:]], axis=0).astype(BF)
        below = jnp.concatenate([near[1, :m], near[1, m:] + ring(far[m:], "y", -1).astype(F32)], axis=0).astype(BF)
    with jax.named_scope("ring"):
        return add(own, ring(above, "y", 1), ring(below, "y", -1))


def chip_groups():
    groups = []
    for core in range(2):
        for group in range(2):
            for z in range(4):
                groups.append([
                    (((x * 4 + y) * 2 + core) * 2 + (group ^ (x & core))) * 4 + z for x in range(2) for y in range(4)
                ])
    return groups


def mm(a, b, ca=1, cb=0):
    return lax.dot_general(a, b, (((ca,), (cb,)), ((), ())), preferred_element_type=F32)


def turn(head, table, back):
    first = head[:, :LANES]
    n = LANES
    left = pltpu.roll(first, n - 32, 1)
    right = pltpu.roll(first, 32, 1)
    sines = left * table[:, n : 2 * n] + right * table[:, 2 * n :]
    first = first * table[:, :n] + (-sines if back else sines)
    return jnp.concatenate([first, head[:, LANES:]], axis=1)


def whole(shape):
    return pl.BlockSpec(shape, lambda *_: (0,) * len(shape), pipeline_mode=pl.Buffered(1))


def kept(shape):
    return pl.BlockSpec(shape, lambda *_: (0,) * len(shape))


def tiles(*shape, axis=0):
    return pl.BlockSpec(shape, lambda i: tuple(i if a == axis else 0 for a in range(len(shape))))


def anywhere(count):
    return [pl.BlockSpec(memory_space=pl.ANY)] * count


TOKEN = jax.ShapeDtypeStruct((1,), F32)


def token_spec():
    return pl.BlockSpec(memory_space=pltpu.SMEM)


def rows_of(*shape, axis=0):
    return pl.BlockSpec(shape, lambda i, s: tuple(i if a == axis else 0 for a in range(len(shape))))


def params():
    return pltpu.CompilerParams(vmem_limit_bytes=VMEM_BYTES)


def part_copies(parts, whole_ref, sems):
    copies, at = [], 0
    for k, part in enumerate(parts):
        n = part.shape[0]
        copies.append(pltpu.make_async_copy(part, whole_ref.at[pl.ds(at, n)], sems.at[k]))
        at += n
    return copies


def call(kernel, name, grid, in_specs, out_specs, out_shape, scratch, flops, size, exps=0):
    return pl.pallas_call(
        kernel,
        grid_spec=pltpu.PrefetchScalarGridSpec(
            num_scalar_prefetch=1, grid=(grid,) if isinstance(grid, int) else grid, in_specs=in_specs, out_specs=[*out_specs, token_spec()], scratch_shapes=scratch
        ),
        out_shape=[*out_shape, TOKEN],
        compiler_params=params(),
        cost_estimate=pl.CostEstimate(flops=0, bytes_accessed=1024, transcendentals=0),
        name=name,
    )


def sds(*shape, dtype=BF):
    return jax.ShapeDtypeStruct(shape, dtype)


def normed(v):
    center = v - jnp.mean(v, axis=-1, keepdims=True)
    return center * lax.rsqrt(jnp.mean(center * center, axis=-1, keepdims=True) + NORM_EPS)


def project_kernel(where, *refs):
    parts, (weights, table) = refs[:8], refs[8:10]
    h1, h2, qkv, norm, b_sum, b_up, token, rows, cols, small, bias, sems = refs[-12:]
    chip = where[0]
    first = pl.program_id(0) == 0
    copies = part_copies(parts, rows, sems)
    load = pltpu.make_async_copy(weights, cols, sems.at[8])
    token[0] = 0.0
    q3 = qkv.shape[1]

    @pl.when(first)
    def _():
        load.start()
        for c in copies:
            c.start()
        load.wait()
        for f in range(16):
            small[f] = cols[f % 2, 0, f // 2, :16, q3:].astype(F32)
            at = slice(f * LANES, (f + 1) * LANES)
            for k, row in enumerate((0, 1, 3, 4)):
                norm[k : k + 1, at] = small[f, row : row + 1]
            b_sum[:, at] = small[f, 2:3] + small[f, 5:6]
        for k in range(6):
            block = (k // 2) * 16 + chip * 2 + k % 2
            bias[:, k * LANES : (k + 1) * LANES] = small[lax.div(block, 3), pl.ds(6 + lax.rem(block, 3), 1), :]
        for k in range(8):
            b_up[:, k * LANES : (k + 1) * LANES] = small[chip * 2 + k // 4, 9 + k % 4 : 10 + k % 4]
        for c in copies:
            c.wait()

    xhat = normed(rows[pl.ds(pl.multiple_of(pl.program_id(0) * TILE, TILE), TILE), :].astype(F32))
    one = (xhat * norm[0:1] + norm[1:2]).astype(BF)
    h1[...] = one
    h2[...] = (xhat * norm[2:3] + norm[3:4]).astype(BF)
    step = cols.shape[3]
    dim = q3 // 3
    mixed = jnp.broadcast_to(bias[...], (TILE, q3))
    for h in range(8):
        mixed += mm(one[:, h * 256 : (h + 1) * 256], cols[:, :, h, :, :q3].reshape(8 * step, -1))
    qkv[:, :dim] = turn(mixed[:, :dim], table[...], False).astype(BF)
    qkv[:, dim : 2 * dim] = turn(mixed[:, dim : 2 * dim], table[...], False).astype(BF)
    qkv[:, 2 * dim :] = mixed[:, 2 * dim :].astype(BF)


def project(where, parts, weights, table, q3, ff, after):
    n, width = 8 * 128, parts[0].shape[1]
    return call(
        project_kernel, "project", n // TILE, [*anywhere(9), rows_of(TILE, 3 * LANES), *anywhere(len(after))],
        [rows_of(TILE, width), rows_of(TILE, width), rows_of(TILE, q3), kept((4, width)), kept((1, width)), kept((1, ff))],
        [sds(n, width), sds(n, width), sds(n, q3), sds(4, width, dtype=F32), sds(1, width, dtype=F32), sds(1, ff, dtype=F32)],
        [
            pltpu.VMEM((n, width), BF), pltpu.VMEM(weights.shape, BF), pltpu.VMEM((16, 16, LANES), F32),
            pltpu.VMEM((1, q3), F32), pltpu.SemaphoreType.DMA((9,)),
        ],
        2 * n * width * q3, 20,
    )(where, *parts, weights, table, *after)


def attend_kernel(where, q, kv, place_q, place_k, doc_q, doc_k, *rest):
    prob, att, token = rest[-3:]
    token[0] = 0.0
    dim = kv.shape[1] // 3
    key, value = kv[:, dim : 2 * dim], kv[:, 2 * dim :]
    scores = mm(q[:, :dim], key, 1, 1) * (dim ** -0.5)
    pq, pk = place_q[...], place_k[...]
    allowed = ((doc_q[...] == doc_k[...]) & (pk <= pq)) | (pk == pq)
    scores = jnp.where(allowed, scores, MASKED)
    expo = jnp.exp(scores - jnp.max(scores, axis=-1, keepdims=True))
    p = (expo * (1.0 / jnp.sum(expo, axis=-1, keepdims=True))).astype(BF)
    prob[...] = p
    out = mm(p, value).astype(BF)
    att[0] = out[:, : dim // 2]
    att[1] = out[:, dim // 2 :]


def attend(where, qkv, places, docs, after):
    n, q3 = qkv.shape
    dim = q3 // 3
    doc_k = jnp.where(docs < 0, -2, docs)
    return call(
        attend_kernel, "attend", n // TILE,
        [rows_of(TILE, q3), whole((n, q3)), rows_of(TILE, 1), whole((1, n)), rows_of(TILE, 1), whole((1, n)), *anywhere(len(after))],
        [rows_of(TILE, n), rows_of(2, TILE, dim // 2, axis=1)], [sds(n, n), sds(2, n, dim // 2)], [],
        4 * n * n * dim, 5, n * n,
    )(where, qkv, qkv, places[:, None], places[None], docs[:, None], doc_k[None], *after)


def expand_kernel(where, h2, weights, bias, *rest):
    act, slope, token, cols, sem = rest[-5:]
    token[0] = 0.0

    @pl.when(pl.program_id(0) == 0)
    def _():
        load = pltpu.make_async_copy(weights, cols, sem)
        load.start()
        load.wait()

    step = cols.shape[3]
    half = act.shape[2]
    for part in range(2):
        at = slice(part * half, (part + 1) * half)
        pre = jnp.broadcast_to(bias[:, at], (TILE, half))
        for h in range(8):
            pre += mm(h2[:, h * 256 : (h + 1) * 256], cols[:, :, h, :, at].reshape(8 * step, -1))
        phi = 0.5 * (1.0 + lax.erf(pre * 0.7071067811865476))
        act[part] = (pre * phi).astype(BF)
        slope[part] = (phi + pre * jnp.exp(-0.5 * pre * pre) * 0.3989422804014327).astype(BF)


def expand(where, h2, weights, bias, after):
    n, width = h2.shape
    ff = weights.shape[-1]
    return call(
        expand_kernel, "expand", n // TILE, [rows_of(TILE, width), *anywhere(1), whole(bias.shape), *anywhere(len(after))],
        [rows_of(2, TILE, ff // 2, axis=1)] * 2, [sds(2, n, ff // 2)] * 2,
        [pltpu.VMEM(weights.shape, BF), pltpu.SemaphoreType.DMA], 2 * n * width * ff, 14, 2 * n * ff,
    )(where, h2, weights, bias, *after)


def branches_kernel(where, act, att, mine, twin, *rest):
    out, token = rest[-2:]
    token[0] = 0.0
    c = where[1]
    first, second = (jnp.concatenate([act[k], att[k]], axis=1) for k in (c, 1 - c))
    total = (mm(first, mine[...]) + mm(second, twin[...])).astype(BF)
    for k in range(2):
        out[where[4 + 2 * pl.program_id(0) + k]] = total[k * 128 : (k + 1) * 128]


def branches_out(where, act, att, mine, twin, after):
    half, tail = act.shape[2], att.shape[2]
    n, width = act.shape[1], mine.shape[1]
    return call(
        branches_kernel, "branches", n // TILE,
        [
            rows_of(2, TILE, half, axis=1), rows_of(2, TILE, tail, axis=1), whole(mine.shape), whole(twin.shape),
            *anywhere(len(after)),
        ],
        [kept((8, 128, width))], [sds(8, 128, width)], [], 4 * n * width * (half + tail), 14,
    )(where, act, att, mine, twin, *after)


def branch_grad_kernel(where, *refs):
    parts, (mine, twin, slope) = refs[:8], refs[8:11]
    g_pre, g_att, bias, token, rows, sems = refs[-6:]
    token[0] = 0.0
    c = where[1]
    half = slope.shape[2]

    @pl.when(pl.program_id(0) == 0)
    def _():
        bias[...] = jnp.zeros_like(bias)
        copies = part_copies(parts, rows, sems)
        for copy in copies:
            copy.start()
        for copy in copies:
            copy.wait()

    g = rows[pl.ds(pl.multiple_of(pl.program_id(0) * TILE, TILE), TILE), :]
    own = mm(g, mine[...], 1, 1)
    other = mm(g, twin[...], 1, 1)
    for at, part in ((c, own), (1 - c, other)):
        pre = (part[:, :half] * slope[at].astype(F32)).astype(BF)
        g_pre[at] = pre
        g_att[at] = part[:, half:].astype(BF)
        bias[at] += jnp.sum(pre.astype(F32), axis=0, keepdims=True)


def branch_grad(where, parts, mine, twin, slope, after):
    n, width = slope.shape[1], mine.shape[1]
    half = slope.shape[2]
    tail = mine.shape[0] - half
    return call(
        branch_grad_kernel, "branch_grad", n // TILE,
        [*anywhere(8), whole(mine.shape), whole(twin.shape), rows_of(2, TILE, half, axis=1), *anywhere(len(after))],
        [rows_of(2, TILE, half, axis=1), rows_of(2, TILE, tail, axis=1), kept((2, 1, half))],
        [sds(2, n, half), sds(2, n, tail), sds(2, 1, half, dtype=F32)],
        [pltpu.VMEM((n, width), BF), pltpu.SemaphoreType.DMA((8,))], 4 * n * width * (half + tail), 16,
    )(where, *parts, mine, twin, slope, *after)


def rows_grad_kernel(where, act, att, *refs):
    parts = refs[:8]
    keep, give, token, rows, sems = refs[-5:]
    token[0] = 0.0

    @pl.when(pl.program_id(0) == 0)
    def _():
        copies = part_copies(parts, rows, sems)
        for copy in copies:
            copy.start()
        for copy in copies:
            copy.wait()

    act_t = mm(act[0], rows[...], 0, 0).astype(BF)
    att_t = mm(att[0], rows[...], 0, 0).astype(BF)
    a, b = act_t.shape[0] // 8, att_t.shape[0] // 8
    for p, out in enumerate((give, keep)):
        @pl.when(pl.program_id(0) == p)
        def _():
            for i in range(8):
                out[i // 4, i % 4, :a] = act_t[i * a : (i + 1) * a]
                out[i // 4, i % 4, a:] = att_t[i * b : (i + 1) * b]


def rows_grad(where, act, att, parts, after):
    n, half, tail, width = act.shape[1], act.shape[2], att.shape[2], parts[0].shape[1]

    def side(p, s):
        return (s[1] * p + (1 - s[1]) * (1 - p), 0, 0)

    return call(
        rows_grad_kernel, "rows_grad", 2,
        [pl.BlockSpec((1, n, half), side), pl.BlockSpec((1, n, tail), side), *anywhere(8 + len(after))],
        [kept((2, 4, (half + tail) // 8, width))] * 2, [sds(2, 4, (half + tail) // 8, width)] * 2,
        [pltpu.VMEM((n, width), BF), pltpu.SemaphoreType.DMA((8,))], 4 * n * width * (half + tail), 14,
    )(where, act, att, *parts, *after)


def attend_back_kernel(where, q, kv, prob, g, table_q, table, *rest):
    out, token, key_sum, value_sum = rest[-4:]
    token[0] = 0.0
    i = pl.program_id(0)
    dim = kv.shape[1] // 3
    key, value = kv[:, dim : 2 * dim], kv[:, 2 * dim :]
    g_tile = jnp.concatenate([g[0], g[1]], axis=1)
    p_low = prob[...]
    p = p_low.astype(F32)
    g_prob = mm(g_tile, value, 1, 1)
    inner = jnp.sum(p * g_prob, axis=-1, keepdims=True)
    g_scores = (p * (g_prob - inner)).astype(BF)
    scale = dim ** -0.5
    g_query = mm(g_scores, key) * scale
    out[pl.ds(i * TILE, TILE), :dim] = turn(g_query, table_q[...], True).astype(BF)
    g_key = mm(g_scores, q[:, :dim], 0, 0)
    g_value = mm(p_low, g_tile, 0, 0)

    @pl.when(i == 0)
    def _():
        key_sum[...] = g_key
        value_sum[...] = g_value

    @pl.when(i > 0)
    def _():
        key_sum[...] += g_key
        value_sum[...] += g_value

    @pl.when(i == pl.num_programs(0) - 1)
    def _():
        out[:, dim : 2 * dim] = turn(key_sum[...] * scale, table[...], True).astype(BF)
        out[:, 2 * dim :] = value_sum[...].astype(BF)


def attend_back(where, qkv, prob, g_att, table, after):
    n, q3 = qkv.shape
    dim = q3 // 3
    return call(
        attend_back_kernel, "attend_back", n // TILE,
        [
            rows_of(TILE, q3), whole((n, q3)), rows_of(TILE, n), rows_of(2, TILE, dim // 2, axis=1), rows_of(TILE, 3 * LANES),
            whole((n, 3 * LANES)), *anywhere(len(after)),
        ],
        [kept((n, q3))], [sds(n, q3)], [pltpu.VMEM((n, dim), F32), pltpu.VMEM((n, dim), F32)], 8 * n * n * dim, 8,
    )(where, qkv, qkv, prob, g_att, table, table, *after)


def partials_kernel(where, *refs):
    parts, (norm, g_mixed, g_pre, w_q, w_u, x_own, out_sum, b_sum, u_bias, dy_sum) = refs[:8], refs[8:18]
    part, layer, token, rows, cols_q, cols_u, sums, sems = refs[-8:]
    token[0] = 0.0
    i = pl.program_id(0)
    copies = part_copies(parts, rows, sems)
    copies += [pltpu.make_async_copy(w_q, cols_q, sems.at[8]), pltpu.make_async_copy(w_u, cols_u, sems.at[9])]

    @pl.when(i == 0)
    def _():
        for copy in copies:
            copy.start()
        sums[...] = jnp.zeros_like(sums)
        layer[...] = (x_own[...].astype(F32) + out_sum[...].astype(F32) + b_sum[...]).astype(BF)
        for copy in copies:
            copy.wait()

    xhat = normed(rows[pl.ds(pl.multiple_of(i * TILE, TILE), TILE), :].astype(F32))
    step = cols_u.shape[3]
    half, q3 = g_pre.shape[2], g_mixed.shape[1]
    gm = g_mixed[...]
    gm_sum = jnp.sum(gm.astype(F32), axis=0, keepdims=True)
    for k in range(3):
        sums[k, 4:5] += gm_sum[:, k * 256 : (k + 1) * 256]
    n = 128
    for h in range(8):
        at = slice(h * 256, (h + 1) * 256)
        wide = cols_u[:, :, h].reshape(8 * step, -1)
        one = mm(gm, cols_q[:, :, h, :, :q3].reshape(8 * step, -1), 1, 1)
        two = mm(g_pre[0], wide[:, :half], 1, 1) + mm(g_pre[1], wide[:, half:], 1, 1)
        e = (one * norm[0:1, at] + two * norm[2:3, at]).astype(BF)
        part[2 * i, :n, at] = e[:n]
        part[2 * i + 1, :n, at] = e[n:]
        xh = xhat[:, at]
        sums[h, 0:1] += jnp.sum(one * xh, axis=0, keepdims=True)
        sums[h, 1:2] += jnp.sum(one, axis=0, keepdims=True)
        sums[h, 2:3] += jnp.sum(two * xh, axis=0, keepdims=True)
        sums[h, 3:4] += jnp.sum(two, axis=0, keepdims=True)

    @pl.when(i == pl.num_programs(0) - 1)
    def _():
        more = part.shape[1] - n
        for slot in range(8):
            to = where[4 + slot]
            row = [sums[to, k : k + 1] for k in range(4)] + [dy_sum[to]]
            for j in range(6):
                block = to * 6 + j
                section, rest = lax.div(block, 16), lax.rem(block, 16)
                value = sums[section, 4:5]
                value = jnp.where(lax.rem(rest, 2) == 0, value[:, :LANES], value[:, LANES:])
                row.append(jnp.where(lax.div(rest, 2) == where[0], value, 0.0))
            row = jnp.concatenate(row, axis=1)
            other = jnp.zeros_like(row)
            if slot == 2:
                other = jnp.concatenate([u_bias[0], u_bias[1], other[:, 2 * half :]], axis=1)
            block = jnp.concatenate([row, other, jnp.zeros((more - 2, row.shape[1]), F32)], axis=0)
            part[slot, n:, :] = block.astype(BF)


def partials(where, parts, norm, g_mixed, g_pre, w_q, w_u, x_own, out_sum, b_sum, u_bias, dy_sum, after):
    n, width = g_mixed.shape[0], norm.shape[1]
    half, q3 = g_pre.shape[2], g_mixed.shape[1]
    return call(
        partials_kernel, "partials", n // TILE,
        [
            *anywhere(8), whole(norm.shape), rows_of(TILE, q3), rows_of(2, TILE, half, axis=1), *anywhere(2),
            *[whole(v.shape) for v in (x_own, out_sum, b_sum, u_bias, dy_sum)], *anywhere(len(after)),
        ],
        [kept((n // 128, 144, width)), kept(x_own.shape)], [sds(n // 128, 144, width), sds(*x_own.shape)],
        [
            pltpu.VMEM((n, width), BF), pltpu.VMEM(w_q.shape, BF), pltpu.VMEM(w_u.shape, BF), pltpu.VMEM((8, 8, 256), F32),
            pltpu.SemaphoreType.DMA((10,)),
        ],
        2 * n * width * (q3 + 2 * half), 24,
    )(where, *parts, norm, g_mixed, g_pre, w_q, w_u, x_own, out_sum, b_sum, u_bias, dy_sum, *after)


def small_out_kernel(where, total, norms, q_bias, u_bias):
    core = where[1]
    for k in range(5):
        pair = [total[0:1, (2 * k + c) * LANES : (2 * k + c + 1) * LANES] for c in range(2)]
        norms[k : k + 1] = jnp.where(core == 0, pair[0], pair[1])
    for j in range(3):
        pair = [total[0:1, (10 + 3 * c + j) * LANES : (11 + 3 * c + j) * LANES] for c in range(2)]
        q_bias[j : j + 1] = jnp.where(core == 0, pair[0], pair[1])
    for j in range(4):
        pair = [total[1:2, (4 * c + j) * LANES : (4 * c + j + 1) * LANES] for c in range(2)]
        u_bias[j : j + 1] = jnp.where(core == 0, pair[0], pair[1])


def small_out(where, total):
    return pl.pallas_call(
        small_out_kernel,
        in_specs=[pl.BlockSpec(memory_space=pltpu.SMEM), pl.BlockSpec(memory_space=pltpu.VMEM)],
        out_specs=[pl.BlockSpec(memory_space=pltpu.VMEM)] * 3,
        out_shape=[jax.ShapeDtypeStruct((n, LANES), F32) for n in (5, 3, 4)],
        name="small_out",
    )(where, total)


def half_grad_kernel(where, left, right, *rest):
    keep, give, token, pair = rest[-4:]
    token[0] = 0.0
    c = where[1]
    n, cols = pair.shape[1:]
    step = n // 4
    done = 0
    for part in range(right.shape[0]):
        res = mm(left[...], right[part], 0, 0).astype(BF)
        w = res.shape[1]
        pair[0, :, done : done + w] = res[:n]
        pair[1, :, done : done + w] = res[n:]
        done += w
    for z in range(4):
        at = slice(z * step, (z + 1) * step)
        keep[z, 0, :, :cols] = pair[c, at]
        give[z, 0, :, :cols] = pair[1 - c, at]
    if keep.shape[-1] > cols:
        keep[:, 0, :, cols:] = rest[0][:, 0]
        give[:, 0, :, cols:] = rest[0][:, 0]


def half_grad(where, left, right, extra, after):
    n, width = left.shape
    cols = right.shape[2] * right.shape[0]
    rows = width // 16
    wide = cols
    more, specs = [], []
    if extra is not None:
        wide += extra.shape[-1]
        more, specs = [extra], [pl.BlockSpec((4, 1, rows // 4, extra.shape[-1]), lambda i, s: (0, i, 0, 0))]
    return call(
        half_grad_kernel, "half_grad", 8,
        [pl.BlockSpec((n, 2 * rows), lambda i, s: (0, i)), whole(right.shape), *specs, *anywhere(len(after))],
        [pl.BlockSpec((4, 1, rows // 4, wide), lambda i, s: (0, i, 0, 0))] * 2, [sds(4, 8, rows // 4, wide)] * 2,
        [pltpu.VMEM((2, rows, cols), BF)], 2 * n * width * cols, 12,
    )(where, left, right, *more, *after)


def columns_out(where, blocks, sections, cols):
    rows, part = blocks[0].shape[2], cols // sections
    width, more = 8 * part, blocks[0].shape[3] - cols

    def kernel(where, *refs):
        out, token = refs[4], refs[-1]
        token[0] = 0.0
        a = pl.program_id(0)
        offset = lax.rem(where[2] - a + 4, 4)
        for k, b in enumerate(refs[:4]):
            @pl.when(offset == k)
            def _():
                for w in range(2):
                    at = jnp.where(where[3] == w, 0, 1)
                    for h in range(8):
                        for s in range(sections):
                            to = s * width + h * part
                            out[w * rows : (w + 1) * rows, to : to + part] = b[at, h, :, s * part : (s + 1) * part].astype(F32)
                    if more:
                        @pl.when(a == 0)
                        def _():
                            refs[5][:, w * rows : (w + 1) * rows] = b[at, :, :, cols:]

    out_specs, out_shape = [rows_of(2 * rows, sections * width)], [sds(8 * rows, sections * width, dtype=F32)]
    if more:
        out_specs.append(kept((8, 2 * rows, more)))
        out_shape.append(sds(8, 2 * rows, more))
    return call(kernel, "columns_out", 4, [whole(b.shape) for b in blocks], out_specs, out_shape, [], 0, 8)(where, *blocks)


def rows_out_kernel(where, mine, twin, down, out, token):
    token[0] = 0.0
    i = pl.program_id(0)
    w, a = lax.div(i, 4), lax.rem(i, 4)
    offset = lax.rem(where[2] - a + 4, 4)
    n = down.shape[0]
    for k, b in enumerate((mine, twin)):
        @pl.when((w == where[3]) == (k == 0))
        def _():
            v = b[offset]
            down[...] = v[:n].astype(F32)
            out[...] = v[n:].astype(F32)


def rows_out(where, mine, twin):
    _, n, width = mine.shape
    cut = n * 4 // 5
    return call(
        rows_out_kernel, "rows_out", 8, [whole(mine.shape), whole(twin.shape)], [rows_of(cut, width), rows_of(n - cut, width)],
        [sds(8 * cut, width, dtype=F32), sds(8 * (n - cut), width, dtype=F32)], [], 0, 8,
    )(where, mine, twin)


def pinned(where, blocks, after):
    def kernel(where, *refs):
        refs[-1][0] = 0.0

    n = len(blocks)
    return pl.pallas_call(
        kernel,
        grid_spec=pltpu.PrefetchScalarGridSpec(
            num_scalar_prefetch=1, grid=(1,), in_specs=anywhere(n + len(after)), out_specs=[*anywhere(n), token_spec()]
        ),
        out_shape=[*[sds(*b.shape) for b in blocks], TOKEN],
        input_output_aliases={1 + k: k for k in range(n)},
        name="pinned",
    )(where, *blocks, *after)[:n]


def pair_sum(keep, give, swap, after=None):
    later = [] if after is None else [after[0]]
    return add(keep, swap(give), *later).astype(BF)


def copies_scatter(pieces, after=None):
    z = lax.axis_index("z")
    later = [] if after is None else [after[0]]

    def piece(offset):
        return lax.dynamic_index_in_dim(pieces, (z + offset) % 4, 0, keepdims=False)

    return add(piece(0), *(ring(piece(o), "z", o) for o in (1, 2, 3)), *later)


def copies_gather(piece):
    return [piece] + [ring(piece, "z", o) for o in (1, 2, 3)]


def over_chips(part, after=None):
    h, n, cols = part.shape
    part = part.reshape(h, 2, n // 2, cols).transpose(1, 0, 2, 3).reshape(2 * h, n // 2, cols)
    part = lax.all_to_all(part, ("w", "x", "y"), 0, 0, tiled=True)
    later = [] if after is None else [after[0]]
    return add(part[:h], part[h:], *later).astype(BF)


def body(
    tokens, segment_ids, out_cotangent, ln1_gain, ln1_bias, qkv_weight, qkv_bias, out_weight, out_bias,
    ln2_gain, ln2_bias, up_weight, up_bias, down_weight, down_bias,
):
    _, shard, width = tokens.shape
    head_dim = width // HEADS
    ff = up_weight.shape[1]
    ff_part = ff // 8
    rows = qkv_weight.shape[0]
    x, y, core, w, z = (lax.axis_index(a) for a in AXES)
    chip = x * 4 + y

    y_offset = jnp.array([1, 3, 0, 2], jnp.int32)
    slot = jnp.arange(8, dtype=jnp.int32)
    slot_chip = (x ^ (slot // 4)) * 4 + (y + y_offset[slot % 4]) % 4
    chip_at = jnp.concatenate([jnp.stack([chip, core, z, w]), slot_chip]).astype(jnp.int32)

    with jax.named_scope("x"):
        x_own = move(tokens[0])
        x_parts = gather(chip_at, x_own)
    with jax.named_scope("ids"):
        ids = move(segment_ids)[0]
    with jax.named_scope("dy"):
        g_own = move(out_cotangent[0])

    step = rows // 4
    q_part, u_part = (lax.dynamic_slice_in_dim(m, z * step, step, 0) for m in (qkv_weight, up_weight))
    q_part = q_part.reshape(step, 3, 8, head_dim).transpose(2, 0, 1, 3).reshape(8, step, 3 * head_dim)
    u_part = u_part.reshape(step, 8, ff_part).transpose(1, 0, 2)
    small = jnp.concatenate([ln1_gain, ln1_bias, out_bias, ln2_gain, ln2_bias, down_bias, qkv_bias, up_bias])
    n_small = small.shape[0] // LANES
    small = jnp.pad(small.reshape(n_small, LANES), ((0, step - n_small), (0, 0)))
    cols = jnp.concatenate([q_part, jnp.broadcast_to(small[None], (8, step, LANES)), u_part], axis=2)
    with jax.named_scope("weights"):
        cols = lax.all_to_all(cols, CHIPS, 0, 0, tiled=True) + x_own[0, 0] * 0
        cut = 3 * head_dim + LANES
        w_q = lax.all_gather(cols[..., :cut], ("c", "z"), axis=0).reshape(2, 4, 8, step, cut)
        w_u = lax.all_gather(cols[..., cut:], ("c", "z"), axis=0).reshape(2, 4, 8, step, ff_part)
    w_mine = jnp.concatenate([down_weight, out_weight], axis=0)
    with jax.named_scope("row_weights"):
        w_twin = swap_core(w_mine)

    group = w ^ (x & core)
    block = ((x ^ (group & core)) ^ (slot // 4)) * 4 + (y - z + y_offset[slot % 4] + 4) % 4
    places = (block[:, None] * shard + jnp.arange(shard, dtype=jnp.int32)[None, :]).reshape(8 * shard)
    half = ROTARY // 2
    lane = jnp.arange(LANES, dtype=jnp.int32)[None]
    freqs = jnp.exp((lane % half).astype(F32) * (-2.0 * math.log(10000.0) / ROTARY))
    angles = places.astype(F32)[:, None] * freqs
    sin = jnp.sin(angles)
    table = jnp.concatenate(
        [
            jnp.where(lane < ROTARY, jnp.cos(angles), 1.0), jnp.where(lane < half, -sin, 0.0),
            jnp.where((lane >= half) & (lane < ROTARY), sin, 0.0),
        ],
        axis=1,
    )
    docs = jnp.take(ids.reshape(8, shard), block, axis=0).reshape(8 * shard)

    (g_own,) = pinned(chip_at, [g_own], (x_parts[3],))
    with jax.named_scope("dy"):
        g_line = gather_line(g_own)
    h1, h2, qkv, norm, b_sum, b_up, _ = project(chip_at, x_parts, w_q, table, 3 * head_dim, ff_part, ())
    g_line = pinned(chip_at, g_line, (qkv,))
    above, below, g_own, far = g_line
    with jax.named_scope("dy/x"):
        g_parts = [*g_line, *[swap_x(b) for b in g_line]]
    prob, attended, _ = attend(chip_at, qkv, places, docs, (above,))
    act, slope, _ = expand(chip_at, h2, w_u, b_up, (attended, g_parts[4], g_parts[5]))
    out_part, _ = branches_out(chip_at, act, attended, w_mine, w_twin, (g_parts[6], g_parts[7]))

    g_pre, g_att, up_bias_grad, _ = branch_grad(chip_at, g_parts, w_mine, w_twin, slope, (out_part,))
    (out_part,) = pinned(chip_at, [out_part], (g_pre,))
    with jax.named_scope("out"):
        out_sum = lax.psum_scatter(out_part, AXES, scatter_dimension=0, axis_index_groups=chip_groups(), tiled=False)
    rows_keep, rows_give, _ = rows_grad(chip_at, act, attended, g_parts, (g_pre, out_part))
    up_keep, up_give, at_up = half_grad(chip_at, h2, g_pre, None, (rows_give,))
    with jax.named_scope("rows/core"):
        rows_part = pair_sum(rows_keep, rows_give, swap_core, at_up)
    g_mixed, at_back = attend_back(chip_at, qkv, prob, g_att, table, (up_give, rows_part))
    with jax.named_scope("up/core"):
        up_part = pair_sum(up_keep, up_give, swap_core, at_back)
    qkv_keep, qkv_give, at_mixed = half_grad(chip_at, h1, g_mixed[None], None, (up_part,))
    with jax.named_scope("rows/w"):
        rows_part = pair_sum(
            lax.dynamic_index_in_dim(rows_part, w, 0, keepdims=False),
            lax.dynamic_index_in_dim(rows_part, 1 - w, 0, keepdims=False), swap_w, at_mixed,
        )
    with jax.named_scope("up/z"):
        up_part = copies_scatter(up_part, at_mixed).astype(BF)
    dy_sum = jnp.sum(g_own.astype(F32), axis=0).reshape(8, 1, 256)
    part, layer_output, last = partials(
        chip_at, x_parts, norm, g_mixed, g_pre, w_q, w_u, x_own, out_sum, b_sum, up_bias_grad, dy_sum,
        (qkv_give, rows_part, up_part),
    )

    with jax.named_scope("up/chips"):
        up_piece = over_chips(up_part, last)
    with jax.named_scope("qkv/core"):
        qkv_part = pair_sum(qkv_keep, qkv_give, swap_core, last)
    with jax.named_scope("qkv/z"):
        qkv_part = copies_scatter(qkv_part).astype(BF)
    with jax.named_scope("qkv/chips"):
        qkv_piece = over_chips(qkv_part)
    with jax.named_scope("qkv/w_back"):
        qkv_both = jnp.stack([qkv_piece, swap_w(qkv_piece)])
    with jax.named_scope("qkv/z_back"):
        qkv_blocks = copies_gather(qkv_both)
    grad_qkv, _ = columns_out(chip_at, qkv_blocks, 3, 3 * head_dim)
    with jax.named_scope("up/w_back"):
        up_both = jnp.stack([up_piece, swap_w(up_piece)])
    (up_both,) = pinned(chip_at, [up_both], (qkv_part,))
    with jax.named_scope("up/z_back"):
        up_blocks = copies_gather(up_both)
    grad_up, _ = columns_out(chip_at, up_blocks, 1, ff_part)
    with jax.named_scope("rows/z"):
        rows_part = copies_scatter(rows_part, last).astype(BF)
    (rows_part,) = pinned(chip_at, [rows_part], (qkv_part,))
    (layer_output,) = pinned(chip_at, [layer_output], (qkv_piece,))
    with jax.named_scope("rows/z_back"):
        rows_part = jnp.stack(copies_gather(rows_part))
    (rows_part,) = pinned(chip_at, [rows_part], (qkv_both,))
    with jax.named_scope("rows/w_back"):
        rows_twin = swap_w(rows_part)
    grad_down, grad_out, _ = rows_out(chip_at, rows_part, rows_twin)
    with jax.named_scope("out/back"):
        layer_output = move_back(layer_output)

    with jax.named_scope("part"):
        total = scatter(part)
    x_rows = x_own.astype(F32)
    center = x_rows - jnp.mean(x_rows, axis=-1, keepdims=True)
    rstd = lax.rsqrt(jnp.mean(center * center, axis=-1, keepdims=True) + NORM_EPS)
    xhat = center * rstd
    e = total[:shard]
    grad_x = rstd * (e - jnp.mean(e, axis=-1, keepdims=True) - xhat * jnp.mean(e * xhat, axis=-1, keepdims=True))
    input_grad = (g_own.astype(F32) + grad_x).astype(BF)
    with jax.named_scope("part/back"):
        input_grad = move_back(input_grad)

    sums = total[shard : shard + 2]
    with jax.named_scope("small"):
        sums = jnp.broadcast_to(sums[None], (16, *sums.shape))
        sums = jnp.sum(lax.all_to_all(sums, ("c", "w", "z"), 0, 0, tiled=True), axis=0)
    norms, grad_qb, grad_ub = small_out(chip_at, sums)

    return (
        layer_output[None], input_grad[None], norms[0], norms[1], grad_qkv, grad_qb.reshape(-1), grad_out,
        norms[4], norms[2], norms[3], grad_up, grad_ub.reshape(-1), grad_down, norms[4],
    )


def solution(mesh):
    fine = Mesh(mesh.devices.reshape(*SIZES.values()), AXES)
    by_owner, by_place = ("x", "y", "c"), ("w", "z")
    act, vec, mat = P(by_owner, by_place, None), P(by_owner), P(by_owner, None)
    return jax.shard_map(
        body,
        mesh=fine,
        in_specs=(act, mat, act, vec, vec, mat, vec, mat, vec, vec, vec, mat, vec, mat, vec),
        out_specs=(act, act, vec, vec, mat, vec, mat, vec, vec, vec, mat, vec, mat, vec),
        check_vma=False,
    )
```

```python
import math

import jax
import jax.numpy as jnp
from jax import lax
from jax.experimental import pallas as pl
from jax.experimental.pallas import tpu as pltpu
from jax.sharding import Mesh, PartitionSpec as P

HEADS = 8
ROTARY = 64
NORM_EPS = 1e-05
MASKED = -1e30
BF = jnp.bfloat16
F32 = jnp.float32
LANES = 128
TILE = 256
VMEM_BYTES = 56 * 1024 * 1024
AXES = ("x", "y", "c", "w", "z")
SIZES = {"x": 2, "y": 4, "c": 2, "w": 2, "z": 4}
CHIPS = ("x", "y")


def pairs_of(axes, target):
    pairs = []
    total = math.prod(SIZES[a] for a in axes)
    for source in range(total):
        rest, at = source, {}
        for a in reversed(axes):
            at[a] = rest % SIZES[a]
            rest //= SIZES[a]
        to, number = {**at, **target(at)}, 0
        for a in axes:
            number = number * SIZES[a] + to[a] % SIZES[a]
        pairs.append((source, number))
    return pairs


def send(block, axes, target):
    return lax.ppermute(block, axes, pairs_of(axes, target))


def place_target(at):
    if at["c"] == 0:
        return {"x": at["w"], "y": at["y"] + at["z"], "w": at["x"], "z": at["y"]}
    return {"x": at["x"] ^ at["w"], "y": at["y"] + at["z"], "z": at["y"]}


MOVES = pairs_of(AXES, place_target)


def move(block):
    return lax.ppermute(block, AXES, MOVES)


def move_back(block):
    return lax.ppermute(block, AXES, [(b, a) for a, b in MOVES])


def swap_core(block):
    return send(block, ("c",), lambda at: {"c": at["c"] ^ 1})


def swap_x(block):
    return send(block, ("x", "c", "w"), lambda at: {"x": at["x"] ^ 1, "w": at["w"] ^ at["c"]})


def swap_w(block):
    return send(block, ("w",), lambda at: {"w": at["w"] ^ 1})


def ring(block, axis, step):
    return send(block, (axis,), lambda at: {axis: at[axis] + step})


def add(*terms):
    return sum(t.astype(F32) for t in terms)


def gather(where, block):
    n = block.shape[0] // 2
    with jax.named_scope("own_x"):
        own_x = swap_x(block)
    with jax.named_scope("ring"):
        above, below = ring(block, "y", -1), ring(block, "y", 1)
    above, below = pinned(where, [above, below], (own_x,))
    with jax.named_scope("far"):
        far = [ring(below[:n], "y", 1), ring(above[n:], "y", -1)]
    with jax.named_scope("near_x"):
        near_x = [swap_x(above), swap_x(below)]
    far = jnp.concatenate(far, axis=0)
    with jax.named_scope("far_x"):
        far_x = swap_x(far)
    return [above, below, block, far, *near_x, own_x, far_x]


def gather_line(block):
    with jax.named_scope("ring"):
        return [ring(block, "y", -1), ring(block, "y", 1), block, ring(block, "y", 2)]


def scatter(part):
    with jax.named_scope("far_x"):
        far = add(part[3], swap_x(part[7])).astype(BF)
    with jax.named_scope("near_x"):
        rest = add(part[:3], swap_x(part[4:7]))
    near, own = rest[:2], rest[2]
    m = far.shape[0] // 2
    with jax.named_scope("far"):
        above = jnp.concatenate([near[0, :m] + ring(far[:m], "y", 1).astype(F32), near[0, m:]], axis=0).astype(BF)
        below = jnp.concatenate([near[1, :m], near[1, m:] + ring(far[m:], "y", -1).astype(F32)], axis=0).astype(BF)
    with jax.named_scope("ring"):
        return add(own, ring(above, "y", 1), ring(below, "y", -1))


def chip_groups():
    groups = []
    for core in range(2):
        for group in range(2):
            for z in range(4):
                groups.append([
                    (((x * 4 + y) * 2 + core) * 2 + (group ^ (x & core))) * 4 + z for x in range(2) for y in range(4)
                ])
    return groups


def mm(a, b, ca=1, cb=0):
    return lax.dot_general(a, b, (((ca,), (cb,)), ((), ())), preferred_element_type=F32)


def turn(head, table, back):
    first = head[:, :LANES]
    n = LANES
    left = pltpu.roll(first, n - 32, 1)
    right = pltpu.roll(first, 32, 1)
    sines = left * table[:, n : 2 * n] + right * table[:, 2 * n :]
    first = first * table[:, :n] + (-sines if back else sines)
    return jnp.concatenate([first, head[:, LANES:]], axis=1)


def whole(shape):
    return pl.BlockSpec(shape, lambda *_: (0,) * len(shape), pipeline_mode=pl.Buffered(1))


def kept(shape):
    return pl.BlockSpec(shape, lambda *_: (0,) * len(shape))


def tiles(*shape, axis=0):
    return pl.BlockSpec(shape, lambda i: tuple(i if a == axis else 0 for a in range(len(shape))))


def anywhere(count):
    return [pl.BlockSpec(memory_space=pl.ANY)] * count


TOKEN = jax.ShapeDtypeStruct((1,), F32)


def token_spec():
    return pl.BlockSpec(memory_space=pltpu.SMEM)


def rows_of(*shape, axis=0):
    return pl.BlockSpec(shape, lambda i, s: tuple(i if a == axis else 0 for a in range(len(shape))))


def params():
    return pltpu.CompilerParams(vmem_limit_bytes=VMEM_BYTES)


def part_copies(parts, whole_ref, sems):
    copies, at = [], 0
    for k, part in enumerate(parts):
        n = part.shape[0]
        copies.append(pltpu.make_async_copy(part, whole_ref.at[pl.ds(at, n)], sems.at[k]))
        at += n
    return copies


def call(kernel, name, grid, in_specs, out_specs, out_shape, scratch, flops, size, exps=0):
    return pl.pallas_call(
        kernel,
        grid_spec=pltpu.PrefetchScalarGridSpec(
            num_scalar_prefetch=1, grid=(grid,) if isinstance(grid, int) else grid, in_specs=in_specs, out_specs=[*out_specs, token_spec()], scratch_shapes=scratch
        ),
        out_shape=[*out_shape, TOKEN],
        compiler_params=params(),
        cost_estimate=pl.CostEstimate(flops=0, bytes_accessed=1024, transcendentals=0),
        name=name,
    )


def sds(*shape, dtype=BF):
    return jax.ShapeDtypeStruct(shape, dtype)


def normed(v):
    center = v - jnp.mean(v, axis=-1, keepdims=True)
    return center * lax.rsqrt(jnp.mean(center * center, axis=-1, keepdims=True) + NORM_EPS)


def project_kernel(where, *refs):
    parts, (weights, table) = refs[:8], refs[8:10]
    h1, h2, qkv, norm, b_sum, b_up, token, rows, cols, small, bias, sems = refs[-12:]
    chip = where[0]
    first = pl.program_id(0) == 0
    copies = part_copies(parts, rows, sems)
    load = pltpu.make_async_copy(weights, cols, sems.at[8])
    token[0] = 0.0
    q3 = qkv.shape[1]

    @pl.when(first)
    def _():
        load.start()
        for c in copies:
            c.start()
        load.wait()
        for f in range(16):
            small[f] = cols[f % 2, 0, f // 2, :16, q3:].astype(F32)
            at = slice(f * LANES, (f + 1) * LANES)
            for k, row in enumerate((0, 1, 3, 4)):
                norm[k : k + 1, at] = small[f, row : row + 1]
            b_sum[:, at] = small[f, 2:3] + small[f, 5:6]
        for k in range(6):
            block = (k // 2) * 16 + chip * 2 + k % 2
            bias[:, k * LANES : (k + 1) * LANES] = small[lax.div(block, 3), pl.ds(6 + lax.rem(block, 3), 1), :]
        for k in range(8):
            b_up[:, k * LANES : (k + 1) * LANES] = small[chip * 2 + k // 4, 9 + k % 4 : 10 + k % 4]
        for c in copies:
            c.wait()

    xhat = normed(rows[pl.ds(pl.multiple_of(pl.program_id(0) * TILE, TILE), TILE), :].astype(F32))
    one = (xhat * norm[0:1] + norm[1:2]).astype(BF)
    h1[...] = one
    h2[...] = (xhat * norm[2:3] + norm[3:4]).astype(BF)
    step = cols.shape[3]
    dim = q3 // 3
    mixed = jnp.broadcast_to(bias[...], (TILE, q3))
    for h in range(8):
        mixed += mm(one[:, h * 256 : (h + 1) * 256], cols[:, :, h, :, :q3].reshape(8 * step, -1))
    qkv[:, :dim] = turn(mixed[:, :dim], table[...], False).astype(BF)
    qkv[:, dim : 2 * dim] = turn(mixed[:, dim : 2 * dim], table[...], False).astype(BF)
    qkv[:, 2 * dim :] = mixed[:, 2 * dim :].astype(BF)


def project(where, parts, weights, table, q3, ff, after):
    n, width = 8 * 128, parts[0].shape[1]
    return call(
        project_kernel, "project", n // TILE, [*anywhere(9), rows_of(TILE, 3 * LANES), *anywhere(len(after))],
        [rows_of(TILE, width), rows_of(TILE, width), rows_of(TILE, q3), kept((4, width)), kept((1, width)), kept((1, ff))],
        [sds(n, width), sds(n, width), sds(n, q3), sds(4, width, dtype=F32), sds(1, width, dtype=F32), sds(1, ff, dtype=F32)],
        [
            pltpu.VMEM((n, width), BF), pltpu.VMEM(weights.shape, BF), pltpu.VMEM((16, 16, LANES), F32),
            pltpu.VMEM((1, q3), F32), pltpu.SemaphoreType.DMA((9,)),
        ],
        2 * n * width * q3, 20,
    )(where, *parts, weights, table, *after)


def attend_kernel(where, q, kv, place_q, place_k, doc_q, doc_k, *rest):
    prob, att, token = rest[-3:]
    token[0] = 0.0
    dim = kv.shape[1] // 3
    key, value = kv[:, dim : 2 * dim], kv[:, 2 * dim :]
    scores = mm(q[:, :dim], key, 1, 1) * (dim ** -0.5)
    pq, pk = place_q[...], place_k[...]
    allowed = ((doc_q[...] == doc_k[...]) & (pk <= pq)) | (pk == pq)
    scores = jnp.where(allowed, scores, MASKED)
    expo = jnp.exp(scores - jnp.max(scores, axis=-1, keepdims=True))
    p = (expo * (1.0 / jnp.sum(expo, axis=-1, keepdims=True))).astype(BF)
    prob[...] = p
    out = mm(p, value).astype(BF)
    att[0] = out[:, : dim // 2]
    att[1] = out[:, dim // 2 :]


def attend(where, qkv, places, docs, after):
    n, q3 = qkv.shape
    dim = q3 // 3
    doc_k = jnp.where(docs < 0, -2, docs)
    return call(
        attend_kernel, "attend", n // TILE,
        [rows_of(TILE, q3), whole((n, q3)), rows_of(TILE, 1), whole((1, n)), rows_of(TILE, 1), whole((1, n)), *anywhere(len(after))],
        [rows_of(TILE, n), rows_of(2, TILE, dim // 2, axis=1)], [sds(n, n), sds(2, n, dim // 2)], [],
        4 * n * n * dim, 5, n * n,
    )(where, qkv, qkv, places[:, None], places[None], docs[:, None], doc_k[None], *after)


def expand_kernel(where, h2, weights, bias, *rest):
    act, slope, token, cols, sem = rest[-5:]
    token[0] = 0.0

    @pl.when(pl.program_id(0) == 0)
    def _():
        load = pltpu.make_async_copy(weights, cols, sem)
        load.start()
        load.wait()

    step = cols.shape[3]
    half = act.shape[2]
    for part in range(2):
        at = slice(part * half, (part + 1) * half)
        pre = jnp.broadcast_to(bias[:, at], (TILE, half))
        for h in range(8):
            pre += mm(h2[:, h * 256 : (h + 1) * 256], cols[:, :, h, :, at].reshape(8 * step, -1))
        phi = 0.5 * (1.0 + lax.erf(pre * 0.7071067811865476))
        act[part] = (pre * phi).astype(BF)
        slope[part] = (phi + pre * jnp.exp(-0.5 * pre * pre) * 0.3989422804014327).astype(BF)


def expand(where, h2, weights, bias, after):
    n, width = h2.shape
    ff = weights.shape[-1]
    return call(
        expand_kernel, "expand", n // TILE, [rows_of(TILE, width), *anywhere(1), whole(bias.shape), *anywhere(len(after))],
        [rows_of(2, TILE, ff // 2, axis=1)] * 2, [sds(2, n, ff // 2)] * 2,
        [pltpu.VMEM(weights.shape, BF), pltpu.SemaphoreType.DMA], 2 * n * width * ff, 14, 2 * n * ff,
    )(where, h2, weights, bias, *after)


def branches_kernel(where, act, att, mine, twin, *rest):
    out, token = rest[-2:]
    token[0] = 0.0
    c = where[1]
    first, second = (jnp.concatenate([act[k], att[k]], axis=1) for k in (c, 1 - c))
    total = (mm(first, mine[...]) + mm(second, twin[...])).astype(BF)
    for k in range(2):
        out[where[4 + 2 * pl.program_id(0) + k]] = total[k * 128 : (k + 1) * 128]


def branches_out(where, act, att, mine, twin, after):
    half, tail = act.shape[2], att.shape[2]
    n, width = act.shape[1], mine.shape[1]
    return call(
        branches_kernel, "branches", n // TILE,
        [
            rows_of(2, TILE, half, axis=1), rows_of(2, TILE, tail, axis=1), whole(mine.shape), whole(twin.shape),
            *anywhere(len(after)),
        ],
        [kept((8, 128, width))], [sds(8, 128, width)], [], 4 * n * width * (half + tail), 14,
    )(where, act, att, mine, twin, *after)


def branch_grad_kernel(where, *refs):
    parts, (mine, twin, slope) = refs[:8], refs[8:11]
    g_pre, g_att, bias, token, rows, sems = refs[-6:]
    token[0] = 0.0
    c = where[1]
    half = slope.shape[2]

    @pl.when(pl.program_id(0) == 0)
    def _():
        bias[...] = jnp.zeros_like(bias)
        copies = part_copies(parts, rows, sems)
        for copy in copies:
            copy.start()
        for copy in copies:
            copy.wait()

    g = rows[pl.ds(pl.multiple_of(pl.program_id(0) * TILE, TILE), TILE), :]
    own = mm(g, mine[...], 1, 1)
    other = mm(g, twin[...], 1, 1)
    for at, part in ((c, own), (1 - c, other)):
        pre = (part[:, :half] * slope[at].astype(F32)).astype(BF)
        g_pre[at] = pre
        g_att[at] = part[:, half:].astype(BF)
        bias[at] += jnp.sum(pre.astype(F32), axis=0, keepdims=True)


def branch_grad(where, parts, mine, twin, slope, after):
    n, width = slope.shape[1], mine.shape[1]
    half = slope.shape[2]
    tail = mine.shape[0] - half
    return call(
        branch_grad_kernel, "branch_grad", n // TILE,
        [*anywhere(8), whole(mine.shape), whole(twin.shape), rows_of(2, TILE, half, axis=1), *anywhere(len(after))],
        [rows_of(2, TILE, half, axis=1), rows_of(2, TILE, tail, axis=1), kept((2, 1, half))],
        [sds(2, n, half), sds(2, n, tail), sds(2, 1, half, dtype=F32)],
        [pltpu.VMEM((n, width), BF), pltpu.SemaphoreType.DMA((8,))], 4 * n * width * (half + tail), 16,
    )(where, *parts, mine, twin, slope, *after)


def rows_grad_kernel(where, act, att, *refs):
    parts = refs[:8]
    keep, give, token, rows, sems = refs[-5:]
    token[0] = 0.0

    @pl.when(pl.program_id(0) == 0)
    def _():
        copies = part_copies(parts, rows, sems)
        for copy in copies:
            copy.start()
        for copy in copies:
            copy.wait()

    act_t = mm(act[0], rows[...], 0, 0).astype(BF)
    att_t = mm(att[0], rows[...], 0, 0).astype(BF)
    a, b = act_t.shape[0] // 8, att_t.shape[0] // 8
    for p, out in enumerate((give, keep)):
        @pl.when(pl.program_id(0) == p)
        def _():
            for i in range(8):
                out[i // 4, i % 4, :a] = act_t[i * a : (i + 1) * a]
                out[i // 4, i % 4, a:] = att_t[i * b : (i + 1) * b]


def rows_grad(where, act, att, parts, after):
    n, half, tail, width = act.shape[1], act.shape[2], att.shape[2], parts[0].shape[1]

    def side(p, s):
        return (s[1] * p + (1 - s[1]) * (1 - p), 0, 0)

    return call(
        rows_grad_kernel, "rows_grad", 2,
        [pl.BlockSpec((1, n, half), side), pl.BlockSpec((1, n, tail), side), *anywhere(8 + len(after))],
        [kept((2, 4, (half + tail) // 8, width))] * 2, [sds(2, 4, (half + tail) // 8, width)] * 2,
        [pltpu.VMEM((n, width), BF), pltpu.SemaphoreType.DMA((8,))], 4 * n * width * (half + tail), 14,
    )(where, act, att, *parts, *after)


def attend_back_kernel(where, q, kv, prob, g, table_q, table, *rest):
    out, token, key_sum, value_sum = rest[-4:]
    token[0] = 0.0
    i = pl.program_id(0)
    dim = kv.shape[1] // 3
    key, value = kv[:, dim : 2 * dim], kv[:, 2 * dim :]
    g_tile = jnp.concatenate([g[0], g[1]], axis=1)
    p_low = prob[...]
    p = p_low.astype(F32)
    g_prob = mm(g_tile, value, 1, 1)
    inner = jnp.sum(p * g_prob, axis=-1, keepdims=True)
    g_scores = (p * (g_prob - inner)).astype(BF)
    scale = dim ** -0.5
    g_query = mm(g_scores, key) * scale
    out[pl.ds(i * TILE, TILE), :dim] = turn(g_query, table_q[...], True).astype(BF)
    g_key = mm(g_scores, q[:, :dim], 0, 0)
    g_value = mm(p_low, g_tile, 0, 0)

    @pl.when(i == 0)
    def _():
        key_sum[...] = g_key
        value_sum[...] = g_value

    @pl.when(i > 0)
    def _():
        key_sum[...] += g_key
        value_sum[...] += g_value

    @pl.when(i == pl.num_programs(0) - 1)
    def _():
        out[:, dim : 2 * dim] = turn(key_sum[...] * scale, table[...], True).astype(BF)
        out[:, 2 * dim :] = value_sum[...].astype(BF)


def attend_back(where, qkv, prob, g_att, table, after):
    n, q3 = qkv.shape
    dim = q3 // 3
    return call(
        attend_back_kernel, "attend_back", n // TILE,
        [
            rows_of(TILE, q3), whole((n, q3)), rows_of(TILE, n), rows_of(2, TILE, dim // 2, axis=1), rows_of(TILE, 3 * LANES),
            whole((n, 3 * LANES)), *anywhere(len(after)),
        ],
        [kept((n, q3))], [sds(n, q3)], [pltpu.VMEM((n, dim), F32), pltpu.VMEM((n, dim), F32)], 8 * n * n * dim, 8,
    )(where, qkv, qkv, prob, g_att, table, table, *after)


def partials_kernel(where, *refs):
    parts, (norm, g_mixed, g_pre, w_q, w_u, x_own, out_sum, b_sum, u_bias, dy_sum) = refs[:8], refs[8:18]
    part, layer, token, rows, cols_q, cols_u, sums, sems = refs[-8:]
    token[0] = 0.0
    i = pl.program_id(0)
    copies = part_copies(parts, rows, sems)
    copies += [pltpu.make_async_copy(w_q, cols_q, sems.at[8]), pltpu.make_async_copy(w_u, cols_u, sems.at[9])]

    @pl.when(i == 0)
    def _():
        for copy in copies:
            copy.start()
        sums[...] = jnp.zeros_like(sums)
        layer[...] = (x_own[...].astype(F32) + out_sum[...].astype(F32) + b_sum[...]).astype(BF)
        for copy in copies:
            copy.wait()

    xhat = normed(rows[pl.ds(pl.multiple_of(i * TILE, TILE), TILE), :].astype(F32))
    step = cols_u.shape[3]
    half, q3 = g_pre.shape[2], g_mixed.shape[1]
    gm = g_mixed[...]
    gm_sum = jnp.sum(gm.astype(F32), axis=0, keepdims=True)
    for k in range(3):
        sums[k, 4:5] += gm_sum[:, k * 256 : (k + 1) * 256]
    n = 128
    for h in range(8):
        at = slice(h * 256, (h + 1) * 256)
        wide = cols_u[:, :, h].reshape(8 * step, -1)
        one = mm(gm, cols_q[:, :, h, :, :q3].reshape(8 * step, -1), 1, 1)
        two = mm(g_pre[0], wide[:, :half], 1, 1) + mm(g_pre[1], wide[:, half:], 1, 1)
        e = (one * norm[0:1, at] + two * norm[2:3, at]).astype(BF)
        part[2 * i, :n, at] = e[:n]
        part[2 * i + 1, :n, at] = e[n:]
        xh = xhat[:, at]
        sums[h, 0:1] += jnp.sum(one * xh, axis=0, keepdims=True)
        sums[h, 1:2] += jnp.sum(one, axis=0, keepdims=True)
        sums[h, 2:3] += jnp.sum(two * xh, axis=0, keepdims=True)
        sums[h, 3:4] += jnp.sum(two, axis=0, keepdims=True)

    @pl.when(i == pl.num_programs(0) - 1)
    def _():
        more = part.shape[1] - n
        for slot in range(8):
            to = where[4 + slot]
            row = [sums[to, k : k + 1] for k in range(4)] + [dy_sum[to]]
            for j in range(6):
                block = to * 6 + j
                section, rest = lax.div(block, 16), lax.rem(block, 16)
                value = sums[section, 4:5]
                value = jnp.where(lax.rem(rest, 2) == 0, value[:, :LANES], value[:, LANES:])
                row.append(jnp.where(lax.div(rest, 2) == where[0], value, 0.0))
            row = jnp.concatenate(row, axis=1)
            other = jnp.zeros_like(row)
            if slot == 2:
                other = jnp.concatenate([u_bias[0], u_bias[1], other[:, 2 * half :]], axis=1)
            block = jnp.concatenate([row, other, jnp.zeros((more - 2, row.shape[1]), F32)], axis=0)
            part[slot, n:, :] = block.astype(BF)


def partials(where, parts, norm, g_mixed, g_pre, w_q, w_u, x_own, out_sum, b_sum, u_bias, dy_sum, after):
    n, width = g_mixed.shape[0], norm.shape[1]
    half, q3 = g_pre.shape[2], g_mixed.shape[1]
    return call(
        partials_kernel, "partials", n // TILE,
        [
            *anywhere(8), whole(norm.shape), rows_of(TILE, q3), rows_of(2, TILE, half, axis=1), *anywhere(2),
            *[whole(v.shape) for v in (x_own, out_sum, b_sum, u_bias, dy_sum)], *anywhere(len(after)),
        ],
        [kept((n // 128, 144, width)), kept(x_own.shape)], [sds(n // 128, 144, width), sds(*x_own.shape)],
        [
            pltpu.VMEM((n, width), BF), pltpu.VMEM(w_q.shape, BF), pltpu.VMEM(w_u.shape, BF), pltpu.VMEM((8, 8, 256), F32),
            pltpu.SemaphoreType.DMA((10,)),
        ],
        2 * n * width * (q3 + 2 * half), 24,
    )(where, *parts, norm, g_mixed, g_pre, w_q, w_u, x_own, out_sum, b_sum, u_bias, dy_sum, *after)


def small_out_kernel(where, total, *rest):
    norms, q_bias, u_bias = rest[-3:]
    core = where[1]
    for k in range(5):
        pair = [total[0:1, (2 * k + c) * LANES : (2 * k + c + 1) * LANES] for c in range(2)]
        norms[k : k + 1] = jnp.where(core == 0, pair[0], pair[1])
    for j in range(3):
        pair = [total[0:1, (10 + 3 * c + j) * LANES : (11 + 3 * c + j) * LANES] for c in range(2)]
        q_bias[j : j + 1] = jnp.where(core == 0, pair[0], pair[1])
    for j in range(4):
        pair = [total[1:2, (4 * c + j) * LANES : (4 * c + j + 1) * LANES] for c in range(2)]
        u_bias[j : j + 1] = jnp.where(core == 0, pair[0], pair[1])


def small_out(where, total, after):
    return pl.pallas_call(
        small_out_kernel,
        in_specs=[pl.BlockSpec(memory_space=pltpu.SMEM), pl.BlockSpec(memory_space=pltpu.VMEM), *anywhere(len(after))],
        out_specs=[pl.BlockSpec(memory_space=pltpu.VMEM)] * 3,
        out_shape=[jax.ShapeDtypeStruct((n, LANES), F32) for n in (5, 3, 4)],
        name="small_out",
    )(where, total, *after)


def half_grad_kernel(where, left, right, *rest):
    keep, give, token, pair = rest[-4:]
    token[0] = 0.0
    c = where[1]
    n, cols = pair.shape[1:]
    step = n // 4
    done = 0
    for part in range(right.shape[0]):
        res = mm(left[...], right[part], 0, 0).astype(BF)
        w = res.shape[1]
        pair[0, :, done : done + w] = res[:n]
        pair[1, :, done : done + w] = res[n:]
        done += w
    for z in range(4):
        at = slice(z * step, (z + 1) * step)
        keep[z, 0, :, :cols] = pair[c, at]
        give[z, 0, :, :cols] = pair[1 - c, at]
    if keep.shape[-1] > cols:
        keep[:, 0, :, cols:] = rest[0][:, 0]
        give[:, 0, :, cols:] = rest[0][:, 0]


def half_grad(where, left, right, extra, after):
    n, width = left.shape
    cols = right.shape[2] * right.shape[0]
    rows = width // 16
    wide = cols
    more, specs = [], []
    if extra is not None:
        wide += extra.shape[-1]
        more, specs = [extra], [pl.BlockSpec((4, 1, rows // 4, extra.shape[-1]), lambda i, s: (0, i, 0, 0))]
    return call(
        half_grad_kernel, "half_grad", 8,
        [pl.BlockSpec((n, 2 * rows), lambda i, s: (0, i)), whole(right.shape), *specs, *anywhere(len(after))],
        [pl.BlockSpec((4, 1, rows // 4, wide), lambda i, s: (0, i, 0, 0))] * 2, [sds(4, 8, rows // 4, wide)] * 2,
        [pltpu.VMEM((2, rows, cols), BF)], 2 * n * width * cols, 12,
    )(where, left, right, *more, *after)


def columns_out(where, blocks, q3):
    _, _, rows, cols = blocks[0].shape
    dim, part = q3 // 3, cols - q3

    def kernel(where, own, below, above, far, far_other, qkv, up, token):
        token[0] = 0.0
        offset = lax.rem(where[2] - pl.program_id(0) + 4, 4)
        for k, pair in enumerate(((own, own), (below, below), (far, far_other), (above, above))):
            @pl.when(offset == k)
            def _():
                for at, ref in enumerate(pair):
                    b = ref if k == 2 else ref.at[at]
                    w = where[3] if at == 0 else 1 - where[3]
                    to_rows = pl.ds(pl.multiple_of(w * rows, rows), rows)
                    for h in range(8):
                        for s in range(3):
                            to = (s * 8 + h) * dim
                            qkv[to_rows, to : to + dim] = b[h, :, s * dim : (s + 1) * dim].astype(F32)
                        up[to_rows, h * part : (h + 1) * part] = b[h, :, q3:].astype(F32)

    return call(
        kernel, "columns_out", 4, [whole(b.shape) for b in blocks], [rows_of(2 * rows, n) for n in (8 * q3, 8 * part)],
        [sds(8 * rows, n, dtype=F32) for n in (8 * q3, 8 * part)], [], 0, 12,
    )(where, *blocks)


def rows_out_kernel(where, mine, twin, down, out, token):
    token[0] = 0.0
    i = pl.program_id(0)
    w, a = lax.div(i, 4), lax.rem(i, 4)
    offset = lax.rem(where[2] - a + 4, 4)
    n = down.shape[0]
    for k, b in enumerate((mine, twin)):
        @pl.when((w == where[3]) == (k == 0))
        def _():
            v = b[offset]
            down[...] = v[:n].astype(F32)
            out[...] = v[n:].astype(F32)


def rows_out(where, mine, twin):
    _, n, width = mine.shape
    cut = n * 4 // 5
    return call(
        rows_out_kernel, "rows_out", 8, [whole(mine.shape), whole(twin.shape)], [rows_of(cut, width), rows_of(n - cut, width)],
        [sds(8 * cut, width, dtype=F32), sds(8 * (n - cut), width, dtype=F32)], [], 0, 8,
    )(where, mine, twin)


def pinned(where, blocks, after):
    def kernel(where, *refs):
        refs[-1][0] = 0.0

    n = len(blocks)
    return pl.pallas_call(
        kernel,
        grid_spec=pltpu.PrefetchScalarGridSpec(
            num_scalar_prefetch=1, grid=(1,), in_specs=anywhere(n + len(after)), out_specs=[*anywhere(n), token_spec()]
        ),
        out_shape=[*[sds(*b.shape) for b in blocks], TOKEN],
        input_output_aliases={1 + k: k for k in range(n)},
        name="pinned",
    )(where, *blocks, *after)[:n]


def pair_sum(keep, give, swap, after=None):
    later = [] if after is None else [after[0]]
    return add(keep, swap(give), *later).astype(BF)


def copies_scatter(pieces, after=None):
    z = lax.axis_index("z")
    later = [] if after is None else [after[0]]

    def piece(offset):
        return lax.dynamic_index_in_dim(pieces, (z + offset) % 4, 0, keepdims=False)

    return add(piece(0), *(ring(piece(o), "z", o) for o in (1, 2, 3)), *later)


def copies_gather(piece):
    return [piece] + [ring(piece, "z", o) for o in (1, 2, 3)]


def over_chips(part, after=None):
    h, n, cols = part.shape
    part = part.reshape(h, 2, n // 2, cols).transpose(1, 0, 2, 3).reshape(2 * h, n // 2, cols)
    part = lax.all_to_all(part, ("w", "x", "y"), 0, 0, tiled=True)
    later = [] if after is None else [after[0]]
    return add(part[:h], part[h:], *later).astype(BF)


def body(
    tokens, segment_ids, out_cotangent, ln1_gain, ln1_bias, qkv_weight, qkv_bias, out_weight, out_bias,
    ln2_gain, ln2_bias, up_weight, up_bias, down_weight, down_bias,
):
    _, shard, width = tokens.shape
    head_dim = width // HEADS
    ff = up_weight.shape[1]
    ff_part = ff // 8
    rows = qkv_weight.shape[0]
    x, y, core, w, z = (lax.axis_index(a) for a in AXES)
    chip = x * 4 + y

    y_offset = jnp.array([1, 3, 0, 2], jnp.int32)
    slot = jnp.arange(8, dtype=jnp.int32)
    slot_chip = (x ^ (slot // 4)) * 4 + (y + y_offset[slot % 4]) % 4
    chip_at = jnp.concatenate([jnp.stack([chip, core, z, w]), slot_chip]).astype(jnp.int32)

    with jax.named_scope("x"):
        x_own = move(tokens[0])
        x_parts = gather(chip_at, x_own)
    with jax.named_scope("ids"):
        ids = move(segment_ids)[0]
    with jax.named_scope("dy"):
        g_own = move(out_cotangent[0])

    step = rows // 4
    q_part, u_part = (lax.dynamic_slice_in_dim(m, z * step, step, 0) for m in (qkv_weight, up_weight))
    q_part = q_part.reshape(step, 3, 8, head_dim).transpose(2, 0, 1, 3).reshape(8, step, 3 * head_dim)
    u_part = u_part.reshape(step, 8, ff_part).transpose(1, 0, 2)
    small = jnp.concatenate([ln1_gain, ln1_bias, out_bias, ln2_gain, ln2_bias, down_bias, qkv_bias, up_bias])
    n_small = small.shape[0] // LANES
    small = jnp.pad(small.reshape(n_small, LANES), ((0, step - n_small), (0, 0)))
    cols = jnp.concatenate([q_part, jnp.broadcast_to(small[None], (8, step, LANES)), u_part], axis=2)
    with jax.named_scope("weights"):
        cols = lax.all_to_all(cols, CHIPS, 0, 0, tiled=True) + x_own[0, 0] * 0
        cut = 3 * head_dim + LANES
        w_q = lax.all_gather(cols[..., :cut], ("c", "z"), axis=0).reshape(2, 4, 8, step, cut)
        w_u = lax.all_gather(cols[..., cut:], ("c", "z"), axis=0).reshape(2, 4, 8, step, ff_part)
    w_mine = jnp.concatenate([down_weight, out_weight], axis=0)
    with jax.named_scope("row_weights"):
        w_twin = swap_core(w_mine)

    group = w ^ (x & core)
    block = ((x ^ (group & core)) ^ (slot // 4)) * 4 + (y - z + y_offset[slot % 4] + 4) % 4
    places = (block[:, None] * shard + jnp.arange(shard, dtype=jnp.int32)[None, :]).reshape(8 * shard)
    half = ROTARY // 2
    lane = jnp.arange(LANES, dtype=jnp.int32)[None]
    freqs = jnp.exp((lane % half).astype(F32) * (-2.0 * math.log(10000.0) / ROTARY))
    angles = places.astype(F32)[:, None] * freqs
    sin = jnp.sin(angles)
    table = jnp.concatenate(
        [
            jnp.where(lane < ROTARY, jnp.cos(angles), 1.0), jnp.where(lane < half, -sin, 0.0),
            jnp.where((lane >= half) & (lane < ROTARY), sin, 0.0),
        ],
        axis=1,
    )
    docs = jnp.take(ids.reshape(8, shard), block, axis=0).reshape(8 * shard)

    (g_own,) = pinned(chip_at, [g_own], (x_parts[3],))
    with jax.named_scope("dy"):
        g_line = gather_line(g_own)
    h1, h2, qkv, norm, b_sum, b_up, _ = project(chip_at, x_parts, w_q, table, 3 * head_dim, ff_part, ())
    g_line = pinned(chip_at, g_line, (qkv,))
    above, below, g_own, far = g_line
    with jax.named_scope("dy/x"):
        g_parts = [*g_line, *[swap_x(b) for b in g_line]]
    prob, attended, _ = attend(chip_at, qkv, places, docs, (above,))
    act, slope, _ = expand(chip_at, h2, w_u, b_up, (attended, g_parts[4], g_parts[5]))
    out_part, _ = branches_out(chip_at, act, attended, w_mine, w_twin, (g_parts[6], g_parts[7]))

    g_pre, g_att, up_bias_grad, _ = branch_grad(chip_at, g_parts, w_mine, w_twin, slope, (out_part,))
    (out_part,) = pinned(chip_at, [out_part], (g_pre,))
    with jax.named_scope("out"):
        out_sum = lax.psum_scatter(out_part, AXES, scatter_dimension=0, axis_index_groups=chip_groups(), tiled=False)
    rows_keep, rows_give, _ = rows_grad(chip_at, act, attended, g_parts, (g_pre, out_part))
    up_keep, up_give, at_up = half_grad(chip_at, h2, g_pre, None, (rows_give,))
    with jax.named_scope("rows/core"):
        rows_part = pair_sum(rows_keep, rows_give, swap_core, at_up)
    g_mixed, at_back = attend_back(chip_at, qkv, prob, g_att, table, (up_give, rows_part))
    with jax.named_scope("up/core"):
        up_part = pair_sum(up_keep, up_give, swap_core, at_back)
    qkv_keep, qkv_give, at_mixed = half_grad(chip_at, h1, g_mixed[None], None, (up_part,))
    with jax.named_scope("rows/w"):
        rows_part = pair_sum(
            lax.dynamic_index_in_dim(rows_part, w, 0, keepdims=False),
            lax.dynamic_index_in_dim(rows_part, 1 - w, 0, keepdims=False), swap_w, at_mixed,
        )
    with jax.named_scope("up/z"):
        up_part = copies_scatter(up_part, at_mixed).astype(BF)
    dy_sum = jnp.sum(g_own.astype(F32), axis=0).reshape(8, 1, 256)
    part, layer_output, last = partials(
        chip_at, x_parts, norm, g_mixed, g_pre, w_q, w_u, x_own, out_sum, b_sum, up_bias_grad, dy_sum,
        (qkv_give, rows_part, up_part),
    )

    with jax.named_scope("qkv/core"):
        qkv_part = pair_sum(qkv_keep, qkv_give, swap_core, last)
    with jax.named_scope("qkv/z"):
        qkv_part = copies_scatter(qkv_part).astype(BF)
    with jax.named_scope("columns/chips"):
        piece = over_chips(jnp.concatenate([qkv_part, up_part], axis=2))
    with jax.named_scope("columns/w_back"):
        qkv_both = jnp.stack([piece, swap_w(piece)])
    with jax.named_scope("columns/z_back"):
        below, above = ring(qkv_both, "z", 1), ring(qkv_both, "z", -1)
    with jax.named_scope("columns/z_far"):
        blocks = [qkv_both, below, above, ring(below[0], "z", 1), ring(above[1], "z", -1)]
    grad_qkv, grad_up, _ = columns_out(chip_at, blocks, 3 * head_dim)
    with jax.named_scope("rows/z"):
        rows_part = copies_scatter(rows_part, last).astype(BF)
    (rows_part,) = pinned(chip_at, [rows_part], (qkv_part,))
    (layer_output,) = pinned(chip_at, [layer_output], (piece,))
    with jax.named_scope("rows/z_back"):
        rows_part = jnp.stack(copies_gather(rows_part))
    (rows_part,) = pinned(chip_at, [rows_part], (qkv_both,))
    with jax.named_scope("rows/w_back"):
        rows_twin = swap_w(rows_part)
    grad_down, grad_out, _ = rows_out(chip_at, rows_part, rows_twin)
    with jax.named_scope("out/back"):
        layer_output = move_back(layer_output)

    with jax.named_scope("part"):
        total = scatter(part)
    x_rows = x_own.astype(F32)
    center = x_rows - jnp.mean(x_rows, axis=-1, keepdims=True)
    rstd = lax.rsqrt(jnp.mean(center * center, axis=-1, keepdims=True) + NORM_EPS)
    xhat = center * rstd
    e = total[:shard]
    grad_x = rstd * (e - jnp.mean(e, axis=-1, keepdims=True) - xhat * jnp.mean(e * xhat, axis=-1, keepdims=True))
    input_grad = (g_own.astype(F32) + grad_x).astype(BF)
    with jax.named_scope("part/back"):
        input_grad = move_back(input_grad)

    sums = total[shard : shard + 2]
    with jax.named_scope("small"):
        sums = jnp.broadcast_to(sums[None], (16, *sums.shape))
        sums = jnp.sum(lax.all_to_all(sums, ("c", "w", "z"), 0, 0, tiled=True), axis=0)
    norms, grad_qb, grad_ub = small_out(chip_at, sums, (grad_qkv, grad_down))

    return (
        layer_output[None], input_grad[None], norms[0], norms[1], grad_qkv, grad_qb.reshape(-1), grad_out,
        norms[4], norms[2], norms[3], grad_up, grad_ub.reshape(-1), grad_down, norms[4],
    )


def solution(mesh):
    fine = Mesh(mesh.devices.reshape(*SIZES.values()), AXES)
    by_owner, by_place = ("x", "y", "c"), ("w", "z")
    act, vec, mat = P(by_owner, by_place, None), P(by_owner), P(by_owner, None)
    return jax.shard_map(
        body,
        mesh=fine,
        in_specs=(act, mat, act, vec, vec, mat, vec, mat, vec, vec, vec, mat, vec, mat, vec),
        out_specs=(act, act, vec, vec, mat, vec, mat, vec, vec, vec, mat, vec, mat, vec),
        check_vma=False,
    )
```

```python
import math

import jax
import jax.numpy as jnp
from jax import lax
from jax.experimental import pallas as pl
from jax.experimental.pallas import tpu as pltpu
from jax.sharding import Mesh, PartitionSpec as P

HEADS = 8
ROTARY = 64
NORM_EPS = 1e-05
MASKED = -1e30
BF = jnp.bfloat16
F32 = jnp.float32
LANES = 128
TILE = 256
VMEM_BYTES = 56 * 1024 * 1024
AXES = ("x", "y", "c", "w", "z")
SIZES = {"x": 2, "y": 4, "c": 2, "w": 2, "z": 4}
CHIPS = ("x", "y")


def pairs_of(axes, target):
    pairs = []
    total = math.prod(SIZES[a] for a in axes)
    for source in range(total):
        rest, at = source, {}
        for a in reversed(axes):
            at[a] = rest % SIZES[a]
            rest //= SIZES[a]
        to, number = {**at, **target(at)}, 0
        for a in axes:
            number = number * SIZES[a] + to[a] % SIZES[a]
        pairs.append((source, number))
    return pairs


def send(block, axes, target):
    return lax.ppermute(block, axes, pairs_of(axes, target))


def place_target(at):
    if at["c"] == 0:
        return {"x": at["w"], "y": at["y"] + at["z"], "w": at["x"], "z": at["y"]}
    return {"x": at["x"] ^ at["w"], "y": at["y"] + at["z"], "z": at["y"]}


MOVES = pairs_of(AXES, place_target)


def move(block):
    return lax.ppermute(block, AXES, MOVES)


def move_back(block):
    return lax.ppermute(block, AXES, [(b, a) for a, b in MOVES])


def swap_core(block):
    return send(block, ("c",), lambda at: {"c": at["c"] ^ 1})


def swap_x(block):
    return send(block, ("x", "c", "w"), lambda at: {"x": at["x"] ^ 1, "w": at["w"] ^ at["c"]})


def swap_w(block):
    return send(block, ("w",), lambda at: {"w": at["w"] ^ 1})


def ring(block, axis, step):
    return send(block, (axis,), lambda at: {axis: at[axis] + step})


def add(*terms):
    return sum(t.astype(F32) for t in terms)


def gather(where, block):
    n = block.shape[0] // 2
    with jax.named_scope("own_x"):
        own_x = swap_x(block)
    with jax.named_scope("ring"):
        above, below = ring(block, "y", -1), ring(block, "y", 1)
    above, below = pinned(where, [above, below], (own_x,))
    with jax.named_scope("far"):
        far = [ring(below[:n], "y", 1), ring(above[n:], "y", -1)]
    with jax.named_scope("near_x"):
        near_x = [swap_x(above), swap_x(below)]
    far = jnp.concatenate(far, axis=0)
    with jax.named_scope("far_x"):
        far_x = swap_x(far)
    return [above, below, block, far, *near_x, own_x, far_x]


def gather_line(block):
    with jax.named_scope("ring"):
        return [ring(block, "y", -1), ring(block, "y", 1), block, ring(block, "y", 2)]


def scatter(part):
    with jax.named_scope("far_x"):
        far = add(part[3], swap_x(part[7])).astype(BF)
    with jax.named_scope("near_x"):
        rest = add(part[:3], swap_x(part[4:7]))
    near, own = rest[:2], rest[2]
    m = far.shape[0] // 2
    with jax.named_scope("far"):
        above = jnp.concatenate([near[0, :m] + ring(far[:m], "y", 1).astype(F32), near[0, m:]], axis=0).astype(BF)
        below = jnp.concatenate([near[1, :m], near[1, m:] + ring(far[m:], "y", -1).astype(F32)], axis=0).astype(BF)
    with jax.named_scope("ring"):
        return add(own, ring(above, "y", 1), ring(below, "y", -1))


def chip_groups():
    groups = []
    for core in range(2):
        for group in range(2):
            for z in range(4):
                groups.append([
                    (((x * 4 + y) * 2 + core) * 2 + (group ^ (x & core))) * 4 + z for x in range(2) for y in range(4)
                ])
    return groups


def mm(a, b, ca=1, cb=0):
    return lax.dot_general(a, b, (((ca,), (cb,)), ((), ())), preferred_element_type=F32)


def turn(head, table, back):
    first = head[:, :LANES]
    n = LANES
    left = pltpu.roll(first, n - 32, 1)
    right = pltpu.roll(first, 32, 1)
    sines = left * table[:, n : 2 * n] + right * table[:, 2 * n :]
    first = first * table[:, :n] + (-sines if back else sines)
    return jnp.concatenate([first, head[:, LANES:]], axis=1)


def whole(shape):
    return pl.BlockSpec(shape, lambda *_: (0,) * len(shape), pipeline_mode=pl.Buffered(1))


def kept(shape):
    return pl.BlockSpec(shape, lambda *_: (0,) * len(shape))


def tiles(*shape, axis=0):
    return pl.BlockSpec(shape, lambda i: tuple(i if a == axis else 0 for a in range(len(shape))))


def anywhere(count):
    return [pl.BlockSpec(memory_space=pl.ANY)] * count


TOKEN = jax.ShapeDtypeStruct((1,), F32)


def token_spec():
    return pl.BlockSpec(memory_space=pltpu.SMEM)


def rows_of(*shape, axis=0):
    return pl.BlockSpec(shape, lambda i, s: tuple(i if a == axis else 0 for a in range(len(shape))))


def params():
    return pltpu.CompilerParams(vmem_limit_bytes=VMEM_BYTES)


def part_copies(parts, whole_ref, sems):
    copies, at = [], 0
    for k, part in enumerate(parts):
        n = part.shape[0]
        copies.append(pltpu.make_async_copy(part, whole_ref.at[pl.ds(at, n)], sems.at[k]))
        at += n
    return copies


def call(kernel, name, grid, in_specs, out_specs, out_shape, scratch, flops, size, exps=0):
    return pl.pallas_call(
        kernel,
        grid_spec=pltpu.PrefetchScalarGridSpec(
            num_scalar_prefetch=1, grid=(grid,) if isinstance(grid, int) else grid, in_specs=in_specs, out_specs=[*out_specs, token_spec()], scratch_shapes=scratch
        ),
        out_shape=[*out_shape, TOKEN],
        compiler_params=params(),
        cost_estimate=pl.CostEstimate(flops=0, bytes_accessed=1024, transcendentals=0),
        name=name,
    )


def sds(*shape, dtype=BF):
    return jax.ShapeDtypeStruct(shape, dtype)


def row_copies(weights, cols, sem):
    step = weights.shape[3]
    return [
        pltpu.make_async_copy(weights.at[c, z, h], cols.at[pl.ds(((h * 2 + c) * 4 + z) * step, step)], sem)
        for h in range(8) for c in range(2) for z in range(4)
    ]


def wait_parts(parts, rows, sems):
    copies = part_copies(parts, rows, sems)
    per = len(parts) // 4
    for k in range(4):
        @pl.when(pl.program_id(0) == k)
        def _():
            for c in copies[k * per : (k + 1) * per]:
                c.wait()


def normed(v):
    center = v - jnp.mean(v, axis=-1, keepdims=True)
    return center * lax.rsqrt(jnp.mean(center * center, axis=-1, keepdims=True) + NORM_EPS)


def project_kernel(where, *refs):
    parts, (weights, table) = refs[:8], refs[8:10]
    h1, h2, qkv, norm, b_sum, b_up, token, rows, cols, small, bias, sems = refs[-12:]
    chip = where[0]
    first = pl.program_id(0) == 0
    copies = part_copies(parts, rows, sems)
    token[0] = 0.0
    q3 = qkv.shape[1]

    @pl.when(first)
    def _():
        for c in row_copies(weights, cols, sems.at[8]):
            c.start()
        for c in copies:
            c.start()
        pltpu.make_async_copy(cols, cols, sems.at[8]).wait()
        for f in range(16):
            small[f] = cols[f * LANES : f * LANES + 16, q3:].astype(F32)
            at = slice(f * LANES, (f + 1) * LANES)
            for k, row in enumerate((0, 1, 3, 4)):
                norm[k : k + 1, at] = small[f, row : row + 1]
            b_sum[:, at] = small[f, 2:3] + small[f, 5:6]
        for k in range(6):
            block = (k // 2) * 16 + chip * 2 + k % 2
            bias[:, k * LANES : (k + 1) * LANES] = small[lax.div(block, 3), pl.ds(6 + lax.rem(block, 3), 1), :]
        for k in range(8):
            b_up[:, k * LANES : (k + 1) * LANES] = small[chip * 2 + k // 4, 9 + k % 4 : 10 + k % 4]

    wait_parts(parts, rows, sems)

    xhat = normed(rows[pl.ds(pl.multiple_of(pl.program_id(0) * TILE, TILE), TILE), :].astype(F32))
    one = (xhat * norm[0:1] + norm[1:2]).astype(BF)
    h1[...] = one
    h2[...] = (xhat * norm[2:3] + norm[3:4]).astype(BF)
    dim = q3 // 3
    mixed = mm(one, cols[:, :q3]) + bias[...]
    qkv[:, :dim] = turn(mixed[:, :dim], table[...], False).astype(BF)
    qkv[:, dim : 2 * dim] = turn(mixed[:, dim : 2 * dim], table[...], False).astype(BF)
    qkv[:, 2 * dim :] = mixed[:, 2 * dim :].astype(BF)


def project(where, parts, weights, table, q3, ff, after):
    n, width = 8 * 128, parts[0].shape[1]
    return call(
        project_kernel, "project", n // TILE, [*anywhere(9), rows_of(TILE, 3 * LANES), *anywhere(len(after))],
        [rows_of(TILE, width), rows_of(TILE, width), rows_of(TILE, q3), kept((4, width)), kept((1, width)), kept((1, ff))],
        [sds(n, width), sds(n, width), sds(n, q3), sds(4, width, dtype=F32), sds(1, width, dtype=F32), sds(1, ff, dtype=F32)],
        [
            pltpu.VMEM((n, width), BF), pltpu.VMEM((width, weights.shape[-1]), BF), pltpu.VMEM((16, 16, LANES), F32),
            pltpu.VMEM((1, q3), F32), pltpu.SemaphoreType.DMA((9,)),
        ],
        2 * n * width * q3, 20,
    )(where, *parts, weights, table, *after)


def attend_kernel(where, q, kv, place_q, place_k, doc_q, doc_k, *rest):
    prob, att, token = rest[-3:]
    token[0] = 0.0
    dim = kv.shape[1] // 3
    key, value = kv[:, dim : 2 * dim], kv[:, 2 * dim :]
    scores = mm(q[:, :dim], key, 1, 1) * (dim ** -0.5)
    pq, pk = place_q[...], place_k[...]
    allowed = ((doc_q[...] == doc_k[...]) & (pk <= pq)) | (pk == pq)
    scores = jnp.where(allowed, scores, MASKED)
    expo = jnp.exp(scores - jnp.max(scores, axis=-1, keepdims=True))
    p = (expo * (1.0 / jnp.sum(expo, axis=-1, keepdims=True))).astype(BF)
    prob[...] = p
    out = mm(p, value).astype(BF)
    att[0] = out[:, : dim // 2]
    att[1] = out[:, dim // 2 :]


def attend(where, qkv, places, docs, after):
    n, q3 = qkv.shape
    dim = q3 // 3
    doc_k = jnp.where(docs < 0, -2, docs)
    return call(
        attend_kernel, "attend", n // TILE,
        [rows_of(TILE, q3), whole((n, q3)), rows_of(TILE, 1), whole((1, n)), rows_of(TILE, 1), whole((1, n)), *anywhere(len(after))],
        [rows_of(TILE, n), rows_of(2, TILE, dim // 2, axis=1)], [sds(n, n), sds(2, n, dim // 2)], [],
        4 * n * n * dim, 5, n * n,
    )(where, qkv, qkv, places[:, None], places[None], docs[:, None], doc_k[None], *after)


def expand_kernel(where, h2, weights, bias, *rest):
    act, slope, token, cols, sem = rest[-5:]
    token[0] = 0.0

    @pl.when(pl.program_id(0) == 0)
    def _():
        for c in row_copies(weights, cols, sem):
            c.start()
        pltpu.make_async_copy(cols, cols, sem).wait()

    half = act.shape[2]
    for part in range(2):
        at = slice(part * half, (part + 1) * half)
        pre = mm(h2[...], cols[:, at]) + bias[:, at]
        phi = 0.5 * (1.0 + lax.erf(pre * 0.7071067811865476))
        act[part] = (pre * phi).astype(BF)
        slope[part] = (phi + pre * jnp.exp(-0.5 * pre * pre) * 0.3989422804014327).astype(BF)


def expand(where, h2, weights, bias, after):
    n, width = h2.shape
    ff = weights.shape[-1]
    return call(
        expand_kernel, "expand", n // TILE, [rows_of(TILE, width), *anywhere(1), whole(bias.shape), *anywhere(len(after))],
        [rows_of(2, TILE, ff // 2, axis=1)] * 2, [sds(2, n, ff // 2)] * 2,
        [pltpu.VMEM((width, ff), BF), pltpu.SemaphoreType.DMA], 2 * n * width * ff, 14, 2 * n * ff,
    )(where, h2, weights, bias, *after)


def branches_kernel(where, act, att, mine, twin, *rest):
    out, token = rest[-2:]
    token[0] = 0.0
    c = where[1]
    first, second = (jnp.concatenate([act[k], att[k]], axis=1) for k in (c, 1 - c))
    total = (mm(first, mine[...]) + mm(second, twin[...])).astype(BF)
    for k in range(2):
        out[where[4 + 2 * pl.program_id(0) + k]] = total[k * 128 : (k + 1) * 128]


def branches_out(where, act, att, mine, twin, after):
    half, tail = act.shape[2], att.shape[2]
    n, width = act.shape[1], mine.shape[1]
    return call(
        branches_kernel, "branches", n // TILE,
        [
            rows_of(2, TILE, half, axis=1), rows_of(2, TILE, tail, axis=1), whole(mine.shape), whole(twin.shape),
            *anywhere(len(after)),
        ],
        [kept((8, 128, width))], [sds(8, 128, width)], [], 4 * n * width * (half + tail), 14,
    )(where, act, att, mine, twin, *after)


def branch_grad_kernel(where, *refs):
    parts, (mine, twin, slope) = refs[:8], refs[8:11]
    g_pre, g_att, bias, token, rows, sems = refs[-6:]
    token[0] = 0.0
    c = where[1]
    half = slope.shape[2]

    @pl.when(pl.program_id(0) == 0)
    def _():
        bias[...] = jnp.zeros_like(bias)
        copies = part_copies(parts, rows, sems)
        for copy in copies:
            copy.start()

    wait_parts(parts, rows, sems)

    g = rows[pl.ds(pl.multiple_of(pl.program_id(0) * TILE, TILE), TILE), :]
    own = mm(g, mine[...], 1, 1)
    other = mm(g, twin[...], 1, 1)
    for at, part in ((c, own), (1 - c, other)):
        pre = (part[:, :half] * slope[at].astype(F32)).astype(BF)
        g_pre[at] = pre
        g_att[at] = part[:, half:].astype(BF)
        bias[at] += jnp.sum(pre.astype(F32), axis=0, keepdims=True)


def branch_grad(where, parts, mine, twin, slope, after):
    n, width = slope.shape[1], mine.shape[1]
    half = slope.shape[2]
    tail = mine.shape[0] - half
    return call(
        branch_grad_kernel, "branch_grad", n // TILE,
        [*anywhere(8), whole(mine.shape), whole(twin.shape), rows_of(2, TILE, half, axis=1), *anywhere(len(after))],
        [rows_of(2, TILE, half, axis=1), rows_of(2, TILE, tail, axis=1), kept((2, 1, half))],
        [sds(2, n, half), sds(2, n, tail), sds(2, 1, half, dtype=F32)],
        [pltpu.VMEM((n, width), BF), pltpu.SemaphoreType.DMA((8,))], 4 * n * width * (half + tail), 16,
    )(where, *parts, mine, twin, slope, *after)


def rows_grad_kernel(where, act, att, *refs):
    parts = refs[:8]
    keep, give, token, rows, sems = refs[-5:]
    token[0] = 0.0

    @pl.when(pl.program_id(0) == 0)
    def _():
        copies = part_copies(parts, rows, sems)
        for copy in copies:
            copy.start()
        for copy in copies:
            copy.wait()

    act_t = mm(act[0], rows[...], 0, 0).astype(BF)
    att_t = mm(att[0], rows[...], 0, 0).astype(BF)
    a, b = act_t.shape[0] // 8, att_t.shape[0] // 8
    for p, out in enumerate((give, keep)):
        @pl.when(pl.program_id(0) == p)
        def _():
            for i in range(8):
                out[i // 4, i % 4, :a] = act_t[i * a : (i + 1) * a]
                out[i // 4, i % 4, a:] = att_t[i * b : (i + 1) * b]


def rows_grad(where, act, att, parts, after):
    n, half, tail, width = act.shape[1], act.shape[2], att.shape[2], parts[0].shape[1]

    def side(p, s):
        return (s[1] * p + (1 - s[1]) * (1 - p), 0, 0)

    return call(
        rows_grad_kernel, "rows_grad", 2,
        [pl.BlockSpec((1, n, half), side), pl.BlockSpec((1, n, tail), side), *anywhere(8 + len(after))],
        [kept((2, 4, (half + tail) // 8, width))] * 2, [sds(2, 4, (half + tail) // 8, width)] * 2,
        [pltpu.VMEM((n, width), BF), pltpu.SemaphoreType.DMA((8,))], 4 * n * width * (half + tail), 14,
    )(where, act, att, *parts, *after)


def attend_back_kernel(where, q, kv, prob, g, table_q, table, *rest):
    out, token, key_sum, value_sum = rest[-4:]
    token[0] = 0.0
    i = pl.program_id(0)
    dim = kv.shape[1] // 3
    key, value = kv[:, dim : 2 * dim], kv[:, 2 * dim :]
    g_tile = jnp.concatenate([g[0], g[1]], axis=1)
    p_low = prob[...]
    p = p_low.astype(F32)
    g_prob = mm(g_tile, value, 1, 1)
    inner = jnp.sum(p * g_prob, axis=-1, keepdims=True)
    g_scores = (p * (g_prob - inner)).astype(BF)
    scale = dim ** -0.5
    g_query = mm(g_scores, key) * scale
    out[pl.ds(i * TILE, TILE), :dim] = turn(g_query, table_q[...], True).astype(BF)
    g_key = mm(g_scores, q[:, :dim], 0, 0)
    g_value = mm(p_low, g_tile, 0, 0)

    @pl.when(i == 0)
    def _():
        key_sum[...] = g_key
        value_sum[...] = g_value

    @pl.when(i > 0)
    def _():
        key_sum[...] += g_key
        value_sum[...] += g_value

    @pl.when(i == pl.num_programs(0) - 1)
    def _():
        out[:, dim : 2 * dim] = turn(key_sum[...] * scale, table[...], True).astype(BF)
        out[:, 2 * dim :] = value_sum[...].astype(BF)


def attend_back(where, qkv, prob, g_att, table, after):
    n, q3 = qkv.shape
    dim = q3 // 3
    return call(
        attend_back_kernel, "attend_back", n // TILE,
        [
            rows_of(TILE, q3), whole((n, q3)), rows_of(TILE, n), rows_of(2, TILE, dim // 2, axis=1), rows_of(TILE, 3 * LANES),
            whole((n, 3 * LANES)), *anywhere(len(after)),
        ],
        [kept((n, q3))], [sds(n, q3)], [pltpu.VMEM((n, dim), F32), pltpu.VMEM((n, dim), F32)], 8 * n * n * dim, 8,
    )(where, qkv, qkv, prob, g_att, table, table, *after)


def partials_kernel(where, *refs):
    parts, (norm, g_mixed, g_pre, w_q, w_u, x_own, out_sum, b_sum, u_bias, dy_sum) = refs[:8], refs[8:18]
    part, layer, token, rows, cols_q, cols_u, sums, sems = refs[-8:]
    token[0] = 0.0
    i = pl.program_id(0)
    copies = part_copies(parts, rows, sems)
    copies += [pltpu.make_async_copy(w_q, cols_q, sems.at[8]), pltpu.make_async_copy(w_u, cols_u, sems.at[9])]

    @pl.when(i == 0)
    def _():
        for copy in copies:
            copy.start()
        sums[...] = jnp.zeros_like(sums)
        layer[...] = (x_own[...].astype(F32) + out_sum[...].astype(F32) + b_sum[...]).astype(BF)
        for copy in copies[8:]:
            copy.wait()

    wait_parts(parts, rows, sems)

    xhat = normed(rows[pl.ds(pl.multiple_of(i * TILE, TILE), TILE), :].astype(F32))
    step = cols_u.shape[3]
    half, q3 = g_pre.shape[2], g_mixed.shape[1]
    gm = g_mixed[...]
    gm_sum = jnp.sum(gm.astype(F32), axis=0, keepdims=True)
    for k in range(3):
        sums[k, 4:5] += gm_sum[:, k * 256 : (k + 1) * 256]
    n = 128
    for h in range(8):
        at = slice(h * 256, (h + 1) * 256)
        wide = cols_u[:, :, h].reshape(8 * step, -1)
        one = mm(gm, cols_q[:, :, h, :, :q3].reshape(8 * step, -1), 1, 1)
        two = mm(g_pre[0], wide[:, :half], 1, 1) + mm(g_pre[1], wide[:, half:], 1, 1)
        e = (one * norm[0:1, at] + two * norm[2:3, at]).astype(BF)
        part[2 * i, :n, at] = e[:n]
        part[2 * i + 1, :n, at] = e[n:]
        xh = xhat[:, at]
        sums[h, 0:1] += jnp.sum(one * xh, axis=0, keepdims=True)
        sums[h, 1:2] += jnp.sum(one, axis=0, keepdims=True)
        sums[h, 2:3] += jnp.sum(two * xh, axis=0, keepdims=True)
        sums[h, 3:4] += jnp.sum(two, axis=0, keepdims=True)

    @pl.when(i == pl.num_programs(0) - 1)
    def _():
        more = part.shape[1] - n
        for slot in range(8):
            to = where[4 + slot]
            row = [sums[to, k : k + 1] for k in range(4)] + [dy_sum[to]]
            for j in range(6):
                block = to * 6 + j
                section, rest = lax.div(block, 16), lax.rem(block, 16)
                value = sums[section, 4:5]
                value = jnp.where(lax.rem(rest, 2) == 0, value[:, :LANES], value[:, LANES:])
                row.append(jnp.where(lax.div(rest, 2) == where[0], value, 0.0))
            row = jnp.concatenate(row, axis=1)
            other = jnp.zeros_like(row)
            if slot == 2:
                other = jnp.concatenate([u_bias[0], u_bias[1], other[:, 2 * half :]], axis=1)
            block = jnp.concatenate([row, other, jnp.zeros((more - 2, row.shape[1]), F32)], axis=0)
            part[slot, n:, :] = block.astype(BF)


def partials(where, parts, norm, g_mixed, g_pre, w_q, w_u, x_own, out_sum, b_sum, u_bias, dy_sum, after):
    n, width = g_mixed.shape[0], norm.shape[1]
    half, q3 = g_pre.shape[2], g_mixed.shape[1]
    return call(
        partials_kernel, "partials", n // TILE,
        [
            *anywhere(8), whole(norm.shape), rows_of(TILE, q3), rows_of(2, TILE, half, axis=1), *anywhere(2),
            *[whole(v.shape) for v in (x_own, out_sum, b_sum, u_bias, dy_sum)], *anywhere(len(after)),
        ],
        [kept((n // 128, 144, width)), kept(x_own.shape)], [sds(n // 128, 144, width), sds(*x_own.shape)],
        [
            pltpu.VMEM((n, width), BF), pltpu.VMEM(w_q.shape, BF), pltpu.VMEM(w_u.shape, BF), pltpu.VMEM((8, 8, 256), F32),
            pltpu.SemaphoreType.DMA((10,)),
        ],
        2 * n * width * (q3 + 2 * half), 24,
    )(where, *parts, norm, g_mixed, g_pre, w_q, w_u, x_own, out_sum, b_sum, u_bias, dy_sum, *after)


def small_out_kernel(where, total, *rest):
    norms, q_bias, u_bias = rest[-3:]
    core = where[1]
    for k in range(5):
        pair = [total[0:1, (2 * k + c) * LANES : (2 * k + c + 1) * LANES] for c in range(2)]
        norms[k : k + 1] = jnp.where(core == 0, pair[0], pair[1])
    for j in range(3):
        pair = [total[0:1, (10 + 3 * c + j) * LANES : (11 + 3 * c + j) * LANES] for c in range(2)]
        q_bias[j : j + 1] = jnp.where(core == 0, pair[0], pair[1])
    for j in range(4):
        pair = [total[1:2, (4 * c + j) * LANES : (4 * c + j + 1) * LANES] for c in range(2)]
        u_bias[j : j + 1] = jnp.where(core == 0, pair[0], pair[1])


def small_out(where, total, after):
    return pl.pallas_call(
        small_out_kernel,
        in_specs=[pl.BlockSpec(memory_space=pltpu.SMEM), pl.BlockSpec(memory_space=pltpu.VMEM), *anywhere(len(after))],
        out_specs=[pl.BlockSpec(memory_space=pltpu.VMEM)] * 3,
        out_shape=[jax.ShapeDtypeStruct((n, LANES), F32) for n in (5, 3, 4)],
        name="small_out",
    )(where, total, *after)


def half_grad_kernel(where, left, right, *rest):
    keep, give, token, pair = rest[-4:]
    token[0] = 0.0
    c = where[1]
    n, cols = pair.shape[1:]
    step = n // 4
    done = 0
    for part in range(right.shape[0]):
        res = mm(left[...], right[part], 0, 0).astype(BF)
        w = res.shape[1]
        pair[0, :, done : done + w] = res[:n]
        pair[1, :, done : done + w] = res[n:]
        done += w
    for z in range(4):
        at = slice(z * step, (z + 1) * step)
        keep[z, 0, :, :cols] = pair[c, at]
        give[z, 0, :, :cols] = pair[1 - c, at]
    if keep.shape[-1] > cols:
        keep[:, 0, :, cols:] = rest[0][:, 0]
        give[:, 0, :, cols:] = rest[0][:, 0]


def half_grad(where, left, right, extra, after):
    n, width = left.shape
    cols = right.shape[2] * right.shape[0]
    rows = width // 16
    wide = cols
    more, specs = [], []
    if extra is not None:
        wide += extra.shape[-1]
        more, specs = [extra], [pl.BlockSpec((4, 1, rows // 4, extra.shape[-1]), lambda i, s: (0, i, 0, 0))]
    return call(
        half_grad_kernel, "half_grad", 8,
        [pl.BlockSpec((n, 2 * rows), lambda i, s: (0, i)), whole(right.shape), *specs, *anywhere(len(after))],
        [pl.BlockSpec((4, 1, rows // 4, wide), lambda i, s: (0, i, 0, 0))] * 2, [sds(4, 8, rows // 4, wide)] * 2,
        [pltpu.VMEM((2, rows, cols), BF)], 2 * n * width * cols, 12,
    )(where, left, right, *more, *after)


def columns_out(where, blocks, q3):
    _, _, rows, cols = blocks[0].shape
    dim, part = q3 // 3, cols - q3

    def kernel(where, own, below, above, far, far_other, qkv, up, token):
        token[0] = 0.0
        offset = lax.rem(where[2] - pl.program_id(0) + 4, 4)
        for k, pair in enumerate(((own, own), (below, below), (far, far_other), (above, above))):
            @pl.when(offset == k)
            def _():
                for at, ref in enumerate(pair):
                    b = ref if k == 2 else ref.at[at]
                    w = where[3] if at == 0 else 1 - where[3]
                    to_rows = pl.ds(pl.multiple_of(w * rows, rows), rows)
                    for h in range(8):
                        for s in range(3):
                            to = (s * 8 + h) * dim
                            qkv[to_rows, to : to + dim] = b[h, :, s * dim : (s + 1) * dim].astype(F32)
                        up[to_rows, h * part : (h + 1) * part] = b[h, :, q3:].astype(F32)

    return call(
        kernel, "columns_out", 4, [whole(b.shape) for b in blocks], [rows_of(2 * rows, n) for n in (8 * q3, 8 * part)],
        [sds(8 * rows, n, dtype=F32) for n in (8 * q3, 8 * part)], [], 0, 12,
    )(where, *blocks)


def rows_out_kernel(where, mine, twin, down, out, token):
    token[0] = 0.0
    n = down.shape[0] // 4
    m = out.shape[0] // 4
    for side, b in enumerate((mine, twin)):
        @pl.when((pl.program_id(0) == where[3]) == (side == 0))
        def _():
            for k in range(4):
                a = lax.rem(where[2] - k + 4, 4)
                down[pl.ds(pl.multiple_of(a * n, n), n)] = b[k, :n].astype(F32)
                out[pl.ds(pl.multiple_of(a * m, m), m)] = b[k, n:].astype(F32)


def rows_out(where, mine, twin):
    _, n, width = mine.shape
    cut = n * 4 // 5
    return call(
        rows_out_kernel, "rows_out", 2, [whole(mine.shape), whole(twin.shape)],
        [rows_of(4 * cut, width), rows_of(4 * (n - cut), width)],
        [sds(8 * cut, width, dtype=F32), sds(8 * (n - cut), width, dtype=F32)], [], 0, 8,
    )(where, mine, twin)


def pinned(where, blocks, after):
    def kernel(where, *refs):
        refs[-1][0] = 0.0

    n = len(blocks)
    return pl.pallas_call(
        kernel,
        grid_spec=pltpu.PrefetchScalarGridSpec(
            num_scalar_prefetch=1, grid=(1,), in_specs=anywhere(n + len(after)), out_specs=[*anywhere(n), token_spec()]
        ),
        out_shape=[*[sds(*b.shape) for b in blocks], TOKEN],
        input_output_aliases={1 + k: k for k in range(n)},
        name="pinned",
    )(where, *blocks, *after)[:n]


def pair_sum(keep, give, swap, after=None):
    later = [] if after is None else [after[0]]
    return add(keep, swap(give), *later).astype(BF)


def copies_scatter(pieces, after=None):
    z = lax.axis_index("z")
    later = [] if after is None else [after[0]]

    def piece(offset):
        return lax.dynamic_index_in_dim(pieces, (z + offset) % 4, 0, keepdims=False)

    return add(piece(0), *(ring(piece(o), "z", o) for o in (1, 2, 3)), *later)


def copies_gather(piece):
    return [piece] + [ring(piece, "z", o) for o in (1, 2, 3)]


def over_chips(part, after=None):
    h, n, cols = part.shape
    part = part.reshape(h, 2, n // 2, cols).transpose(1, 0, 2, 3).reshape(2 * h, n // 2, cols)
    part = lax.all_to_all(part, ("w", "x", "y"), 0, 0, tiled=True)
    later = [] if after is None else [after[0]]
    return add(part[:h], part[h:], *later).astype(BF)


def body(
    tokens, segment_ids, out_cotangent, ln1_gain, ln1_bias, qkv_weight, qkv_bias, out_weight, out_bias,
    ln2_gain, ln2_bias, up_weight, up_bias, down_weight, down_bias,
):
    _, shard, width = tokens.shape
    head_dim = width // HEADS
    ff = up_weight.shape[1]
    ff_part = ff // 8
    rows = qkv_weight.shape[0]
    x, y, core, w, z = (lax.axis_index(a) for a in AXES)
    chip = x * 4 + y

    y_offset = jnp.array([1, 3, 0, 2], jnp.int32)
    slot = jnp.arange(8, dtype=jnp.int32)
    slot_chip = (x ^ (slot // 4)) * 4 + (y + y_offset[slot % 4]) % 4
    chip_at = jnp.concatenate([jnp.stack([chip, core, z, w]), slot_chip]).astype(jnp.int32)

    with jax.named_scope("x"):
        x_own = move(tokens[0])
        x_parts = gather(chip_at, x_own)
    with jax.named_scope("ids"):
        ids = move(segment_ids)[0]
    with jax.named_scope("dy"):
        g_own = move(out_cotangent[0])

    step = rows // 4
    q_part, u_part = (lax.dynamic_slice_in_dim(m, z * step, step, 0) for m in (qkv_weight, up_weight))
    q_part = q_part.reshape(step, 3, 8, head_dim).transpose(2, 0, 1, 3).reshape(8, step, 3 * head_dim)
    u_part = u_part.reshape(step, 8, ff_part).transpose(1, 0, 2)
    small = jnp.concatenate([ln1_gain, ln1_bias, out_bias, ln2_gain, ln2_bias, down_bias, qkv_bias, up_bias])
    n_small = small.shape[0] // LANES
    small = jnp.pad(small.reshape(n_small, LANES), ((0, step - n_small), (0, 0)))
    cols = jnp.concatenate([q_part, jnp.broadcast_to(small[None], (8, step, LANES)), u_part], axis=2)
    with jax.named_scope("weights"):
        cols = lax.all_to_all(cols, CHIPS, 0, 0, tiled=True) + x_own[0, 0] * 0
        cut = 3 * head_dim + LANES
        w_q = lax.all_gather(cols[..., :cut], ("c", "z"), axis=0).reshape(2, 4, 8, step, cut)
        w_u = lax.all_gather(cols[..., cut:], ("c", "z"), axis=0).reshape(2, 4, 8, step, ff_part)
    w_mine = jnp.concatenate([down_weight, out_weight], axis=0)
    with jax.named_scope("row_weights"):
        w_twin = swap_core(w_mine)

    group = w ^ (x & core)
    block = ((x ^ (group & core)) ^ (slot // 4)) * 4 + (y - z + y_offset[slot % 4] + 4) % 4
    places = (block[:, None] * shard + jnp.arange(shard, dtype=jnp.int32)[None, :]).reshape(8 * shard)
    half = ROTARY // 2
    lane = jnp.arange(LANES, dtype=jnp.int32)[None]
    freqs = jnp.exp((lane % half).astype(F32) * (-2.0 * math.log(10000.0) / ROTARY))
    angles = places.astype(F32)[:, None] * freqs
    sin = jnp.sin(angles)
    table = jnp.concatenate(
        [
            jnp.where(lane < ROTARY, jnp.cos(angles), 1.0), jnp.where(lane < half, -sin, 0.0),
            jnp.where((lane >= half) & (lane < ROTARY), sin, 0.0),
        ],
        axis=1,
    )
    docs = jnp.take(ids.reshape(8, shard), block, axis=0).reshape(8 * shard)

    (g_own,) = pinned(chip_at, [g_own], (x_parts[3],))
    with jax.named_scope("dy"):
        g_line = gather_line(g_own)
    h1, h2, qkv, norm, b_sum, b_up, _ = project(chip_at, x_parts, w_q, table, 3 * head_dim, ff_part, ())
    g_line = pinned(chip_at, g_line, (qkv,))
    above, below, g_own, far = g_line
    with jax.named_scope("dy/x"):
        g_parts = [*g_line, *[swap_x(b) for b in g_line]]
    prob, attended, _ = attend(chip_at, qkv, places, docs, (above,))
    act, slope, _ = expand(chip_at, h2, w_u, b_up, (attended, g_parts[4], g_parts[5]))
    out_part, _ = branches_out(chip_at, act, attended, w_mine, w_twin, (g_parts[6], g_parts[7]))

    g_pre, g_att, up_bias_grad, _ = branch_grad(chip_at, g_parts, w_mine, w_twin, slope, (out_part,))
    (out_part,) = pinned(chip_at, [out_part], (g_pre,))
    with jax.named_scope("out"):
        out_sum = lax.psum_scatter(out_part, AXES, scatter_dimension=0, axis_index_groups=chip_groups(), tiled=False)
    rows_keep, rows_give, _ = rows_grad(chip_at, act, attended, g_parts, (g_pre, out_part))
    up_keep, up_give, at_up = half_grad(chip_at, h2, g_pre, None, (rows_give,))
    with jax.named_scope("rows/core"):
        rows_part = pair_sum(rows_keep, rows_give, swap_core, at_up)
    g_mixed, at_back = attend_back(chip_at, qkv, prob, g_att, table, (up_give, rows_part))
    with jax.named_scope("up/core"):
        up_part = pair_sum(up_keep, up_give, swap_core, at_back)
    qkv_keep, qkv_give, at_mixed = half_grad(chip_at, h1, g_mixed[None], None, (up_part,))
    with jax.named_scope("rows/w"):
        rows_part = pair_sum(
            lax.dynamic_index_in_dim(rows_part, w, 0, keepdims=False),
            lax.dynamic_index_in_dim(rows_part, 1 - w, 0, keepdims=False), swap_w, at_mixed,
        )
    with jax.named_scope("up/z"):
        up_part = copies_scatter(up_part, at_mixed).astype(BF)
    dy_sum = jnp.sum(g_own.astype(F32), axis=0).reshape(8, 1, 256)
    part, layer_output, last = partials(
        chip_at, x_parts, norm, g_mixed, g_pre, w_q, w_u, x_own, out_sum, b_sum, up_bias_grad, dy_sum,
        (qkv_give, rows_part, up_part),
    )

    with jax.named_scope("qkv/core"):
        qkv_part = pair_sum(qkv_keep, qkv_give, swap_core, last)
    with jax.named_scope("qkv/z"):
        qkv_part = copies_scatter(qkv_part).astype(BF)
    with jax.named_scope("columns/chips"):
        piece = over_chips(jnp.concatenate([qkv_part, up_part], axis=2))
    with jax.named_scope("columns/w_back"):
        qkv_both = jnp.stack([piece, swap_w(piece)])
    with jax.named_scope("columns/z_back"):
        below, above = ring(qkv_both, "z", 1), ring(qkv_both, "z", -1)
    with jax.named_scope("columns/z_far"):
        blocks = [qkv_both, below, above, ring(below[0], "z", 1), ring(above[1], "z", -1)]
    grad_qkv, grad_up, _ = columns_out(chip_at, blocks, 3 * head_dim)
    with jax.named_scope("rows/z"):
        rows_part = copies_scatter(rows_part, last).astype(BF)
    (rows_part,) = pinned(chip_at, [rows_part], (qkv_part,))
    (layer_output,) = pinned(chip_at, [layer_output], (piece,))
    with jax.named_scope("rows/z_back"):
        rows_part = jnp.stack(copies_gather(rows_part))
    (rows_part,) = pinned(chip_at, [rows_part], (qkv_both,))
    with jax.named_scope("rows/w_back"):
        rows_twin = swap_w(rows_part)
    grad_down, grad_out, _ = rows_out(chip_at, rows_part, rows_twin)
    with jax.named_scope("out/back"):
        layer_output = move_back(layer_output)

    with jax.named_scope("part"):
        total = scatter(part)
    x_rows = x_own.astype(F32)
    center = x_rows - jnp.mean(x_rows, axis=-1, keepdims=True)
    rstd = lax.rsqrt(jnp.mean(center * center, axis=-1, keepdims=True) + NORM_EPS)
    xhat = center * rstd
    e = total[:shard]
    grad_x = rstd * (e - jnp.mean(e, axis=-1, keepdims=True) - xhat * jnp.mean(e * xhat, axis=-1, keepdims=True))
    input_grad = (g_own.astype(F32) + grad_x).astype(BF)
    with jax.named_scope("part/back"):
        input_grad = move_back(input_grad)

    sums = total[shard : shard + 2]
    with jax.named_scope("small"):
        sums = jnp.broadcast_to(sums[None], (16, *sums.shape))
        sums = jnp.sum(lax.all_to_all(sums, ("c", "w", "z"), 0, 0, tiled=True), axis=0)
    norms, grad_qb, grad_ub = small_out(chip_at, sums, (grad_qkv, grad_down))

    return (
        layer_output[None], input_grad[None], norms[0], norms[1], grad_qkv, grad_qb.reshape(-1), grad_out,
        norms[4], norms[2], norms[3], grad_up, grad_ub.reshape(-1), grad_down, norms[4],
    )


def solution(mesh):
    fine = Mesh(mesh.devices.reshape(*SIZES.values()), AXES)
    by_owner, by_place = ("x", "y", "c"), ("w", "z")
    act, vec, mat = P(by_owner, by_place, None), P(by_owner), P(by_owner, None)
    return jax.shard_map(
        body,
        mesh=fine,
        in_specs=(act, mat, act, vec, vec, mat, vec, mat, vec, vec, vec, mat, vec, mat, vec),
        out_specs=(act, act, vec, vec, mat, vec, mat, vec, vec, vec, mat, vec, mat, vec),
        check_vma=False,
    )
```
